32 devices in a mesh: dp: 8 (over z, x), tensor: 4 (over y, core).
Axes of the slice: x: 2, y: 2, z: 4, core: 2. Of those that a mesh axis runs over, the one named last changes fastest.
Arguments:
- hidden_in: bfloat16 [4096, 2048], P(('dp', 'tensor')), may hold values from -6 to 6
- out_grad: bfloat16 [4096, 2048], P(('dp', 'tensor')), may hold values from -6 to 6
- w_query: bfloat16 [2048, 2048], P('dp', 'tensor'), may hold values from -0.125 to 0.125
- w_key: bfloat16 [2048, 2048], P('dp', 'tensor'), may hold values from -0.125 to 0.125
- w_value: bfloat16 [2048, 2048], P('dp', 'tensor'), may hold values from -0.125 to 0.125
- w_out: bfloat16 [2048, 2048], P('dp', 'tensor'), may hold values from -0.125 to 0.125
- w_gate: bfloat16 [2048, 8192], P('dp', 'tensor'), may hold values from -0.125 to 0.125
- w_up: bfloat16 [2048, 8192], P('dp', 'tensor'), may hold values from -0.125 to 0.125
- w_down: bfloat16 [2048, 8192], P('dp', 'tensor'), may hold values from -0.0625 to 0.0625
- gains: float32 [4, 2048], replicated, may hold values from 0.25 to 1.75
- seg_ids: int32 [4096], P('dp'), may hold values from 0 to 63, as said below
- positions: int32 [4096], P('dp'), may hold values from 0 to 511, as said below
Outputs:
- hidden_out: bfloat16 [4096, 2048], P(('dp', 'tensor'))
- in_grad: float32 [4096, 2048], P(('dp', 'tensor'))
- w_query_grad: float32 [2048, 2048], P('dp', 'tensor')
- w_key_grad: float32 [2048, 2048], P('dp', 'tensor')
- w_value_grad: float32 [2048, 2048], P('dp', 'tensor')
- w_out_grad: float32 [2048, 2048], P('dp', 'tensor')
- w_gate_grad: float32 [2048, 8192], P('dp', 'tensor')
- w_up_grad: float32 [2048, 8192], P('dp', 'tensor')
- w_down_grad: float32 [2048, 8192], P('dp', 'tensor')
- gains_grad: float32 [4, 2048], replicated
The draws below stay inside these ranges and needn't reach their ends.
Inputs may be any that keep to these rules, and one draw needn't show every extreme that they name: Within each sequence of 512 consecutive tokens, seg_ids start at 0 and never fall; each id marks one document; documents start only at tokens whose index within the sequence is a multiple of 8. positions count 0, 1, 2, ... from the first token of each document.
All inputs are finite; a program needn't handle non-finite values.
Results may differ from the reference program's by a relative error of at most 0.02.
Values may be sent and summed in bfloat16 or wider, within the bound.
No kernel may reach another device: no remote copies, remote signals or barrier semaphores. Data moves between devices by JAX's collectives and lax.ppermute only.
A program may use at most 320 MiB of HBM per device.

```python
import jax
import jax.numpy as jnp
from jax import lax

D = 2048
HEADS = 16
HEAD_DIM = 128
FF = 8192
SEQ = 512
TOKENS = 4096


def documents(key):
    base_key = jax.random.fold_in(key, 11)
    rate_key, cut_key = jax.random.split(base_key)
    n_seq = TOKENS // SEQ
    rate_class = jax.random.randint(rate_key, (n_seq, 1), 0, 4)
    ticket = jax.random.randint(cut_key, (n_seq, SEQ), 0, 1 << 20)
    limit = jnp.right_shift(jnp.full((n_seq, 1), 1 << 20, jnp.int32), 1 + 2 * rate_class)
    place = jnp.arange(SEQ, dtype=jnp.int32)[None, :]
    seq_index = jnp.arange(n_seq, dtype=jnp.int32)[:, None]
    allowed = place % 8 == 0
    starts = allowed & (ticket < limit) | (place == 0) | allowed & (seq_index == n_seq - 1)
    starts = starts & jnp.logical_not((seq_index == 0) & (place > 0))
    seg_rows = jnp.cumsum(starts.astype(jnp.int32), axis=1) - 1
    first_place = lax.cummax(jnp.where(starts, place, 0), axis=1)
    return (seg_rows.reshape(-1).astype(jnp.int32), (place - first_place).reshape(-1).astype(jnp.int32))


def draw_seg_ids(key, part):
    return documents(key)[0]


def draw_positions(key, part):
    return documents(key)[1]


def shard_levels(rng, extent, shards, smallest, largest):
    factor_of, own = 1.0, jax.random.fold_in(rng, 6)
    for position, shards_of in shards:
        heights = jnp.exp(jax.random.uniform(jax.random.fold_in(own, position), (shards_of,), jnp.float32, smallest / len(shards), largest / len(shards)))
        factor_of = factor_of * jnp.repeat(heights, extent[position] // shards_of).reshape([-1 if axis == position else 1 for axis in range(len(extent))])
    return factor_of


def bell_draw(rng, extent, deviation, reach, cuts=(), kind=jnp.bfloat16):
    entries = jax.random.normal(rng, extent, jnp.float32) * deviation
    if len(cuts) > 0:
        entries = shard_levels(rng, extent, cuts, -0.22, 0.18) * entries
    return jnp.clip(entries, min=-reach, max=reach).astype(kind)


def setup_inputs(seed: int = 0) -> dict:
    arg_keys = jax.random.split(jax.random.key(seed), 13)
    hidden_in = bell_draw(arg_keys[0], (TOKENS, D), 1.0, 6.0, ((0, 32),))
    out_grad = bell_draw(arg_keys[1], (TOKENS, D), 1.0, 6.0, ((0, 32),))
    w_query = bell_draw(arg_keys[2], (D, D), D ** -0.5, 0.125, ((0, 8), (1, 4)))
    w_key = bell_draw(arg_keys[3], (D, D), D ** -0.5, 0.125, ((0, 8), (1, 4)))
    w_value = bell_draw(arg_keys[4], (D, D), D ** -0.5, 0.125, ((0, 8), (1, 4)))
    w_out = bell_draw(arg_keys[5], (D, D), D ** -0.5, 0.125, ((0, 8), (1, 4)))
    w_gate = bell_draw(arg_keys[6], (D, FF), D ** -0.5, 0.125, ((0, 8), (1, 4)))
    w_up = bell_draw(arg_keys[7], (D, FF), D ** -0.5, 0.125, ((0, 8), (1, 4)))
    w_down = bell_draw(arg_keys[8], (D, FF), FF ** -0.5, 0.0625, ((0, 8), (1, 4)))
    gains = jnp.clip(1.0 + 0.15 * jax.random.normal(arg_keys[9], (4, D), jnp.float32), 0.25, 1.75)
    seg_ids = draw_seg_ids(jax.random.fold_in(arg_keys[12], 71), 0)
    positions = draw_positions(jax.random.fold_in(arg_keys[12], 71), 0)
    return {"hidden_in": hidden_in, "out_grad": out_grad, "w_query": w_query, "w_key": w_key, "w_value": w_value, "w_out": w_out, "w_gate": w_gate, "w_up": w_up, "w_down": w_down, "gains": gains, "seg_ids": seg_ids, "positions": positions}


@jax.custom_vjp
def low(v):
    return lax.optimization_barrier(v.astype(jnp.bfloat16)).astype(jnp.float32)

@jax.custom_vjp
def low_back(v):
    return v

def low_keep(v):
    return (low(v), None)

def low_pass(kept, grad):
    return (grad,)

def back_keep(v):
    return (v, None)

def back_low(kept, grad):
    return (low(grad),)
low.defvjp(low_keep, low_pass)
low_back.defvjp(back_keep, back_low)
EPS = 1e-06
THETA = 500000.0
NEG = -1e+30
PRECISE = lax.Precision.HIGHEST

def matmul_high(left_mat, right_mat):
    return jnp.dot(left_mat, right_mat, precision=PRECISE, preferred_element_type=jnp.float32)

def rms_scale(values, gain_row):
    return values * lax.rsqrt(lax.optimization_barrier(jnp.mean(values * values, -1, keepdims=True)) + EPS) * gain_row

def rope_tables(pos_row, head_dim):
    half_dim = head_dim // 2
    inverse = THETA ** (-(jnp.arange(half_dim, dtype=jnp.float32) * 2.0 / head_dim))
    angles = pos_row.astype(jnp.float32)[:, None] * inverse[None, :]
    return (jnp.cos(angles)[:, None, :], jnp.sin(angles)[:, None, :])

def rotate(values, cos_tab, sin_tab):
    half_dim = values.shape[-1] // 2
    first_half, second_half = (values[..., :half_dim], values[..., half_dim:])
    return jnp.concatenate([first_half * cos_tab - second_half * sin_tab, second_half * cos_tab + first_half * sin_tab], -1)

def block_forward(hidden, weights, seg_row, pos_row):
    w_query, w_key, w_value, w_out, w_gate, w_up, w_down, gains = weights
    seq_len = hidden.shape[0]
    queries = low_back(matmul_high(hidden, w_query))
    key_proj = low_back(matmul_high(hidden, w_key))
    value_proj = low(low_back(matmul_high(hidden, w_value)))
    cos_tab, sin_tab = rope_tables(pos_row, HEAD_DIM)
    q_rot = low(rotate(rms_scale(queries, gains[0]).reshape(seq_len, HEADS, HEAD_DIM), cos_tab, sin_tab))
    k_rot = low(rotate(rms_scale(key_proj, gains[1]).reshape(seq_len, HEADS, HEAD_DIM), cos_tab, sin_tab))
    v_heads = value_proj.reshape(seq_len, HEADS, HEAD_DIM)
    token_ids = jnp.arange(seq_len)
    same_doc = (seg_row[:, None] == seg_row[None, :]) & (token_ids[:, None] >= token_ids[None, :])
    score_scale = HEAD_DIM ** (-0.5)

    def one_head(operands):
        q_head, k_head, v_head = operands
        scores = low_back(matmul_high(q_head, k_head.T) * score_scale)
        scores = jnp.where(same_doc, scores, NEG)
        probs = low(jax.nn.softmax(scores, -1))
        return low(low_back(matmul_high(probs, v_head)))
    attended = lax.map(jax.checkpoint(one_head), (q_rot.transpose(1, 0, 2), k_rot.transpose(1, 0, 2), v_heads.transpose(1, 0, 2)))
    attended = attended.transpose(1, 0, 2).reshape(seq_len, HEADS * HEAD_DIM)
    attn_sum = low_back(matmul_high(attended, w_out.T))
    resid = hidden + rms_scale(attn_sum, gains[2])
    mlp_in = low(resid)
    gate_proj = low_back(matmul_high(mlp_in, w_gate))
    up_proj = low_back(matmul_high(mlp_in, w_up))
    hidden_act = low(jax.nn.silu(gate_proj) * up_proj)
    mlp_sum = low_back(matmul_high(hidden_act, w_down.T))
    return resid + rms_scale(mlp_sum, gains[3])

def reference(hidden_in, out_grad, w_query, w_key, w_value, w_out, w_gate, w_up, w_down, gains, seg_ids, positions):
    weights = tuple((weight_arr.astype(jnp.float32) for weight_arr in (w_query, w_key, w_value, w_out, w_gate, w_up, w_down, gains)))
    n_seq = TOKENS // SEQ
    inputs = hidden_in.astype(jnp.float32).reshape(n_seq, SEQ, D)
    cotangents = out_grad.astype(jnp.float32).reshape(n_seq, SEQ, D)
    seg_rows = seg_ids.reshape(n_seq, SEQ)
    pos_rows = positions.reshape(n_seq, SEQ)

    def one_sequence(acc, item):
        hidden, cotangent, seg_row, pos_row = item
        result, pull = jax.vjp(lambda hid, wts: block_forward(hid, wts, seg_row, pos_row), hidden, weights)
        grad_hidden, grad_weights = pull(cotangent)
        acc = jax.tree.map(lambda total_g, new_g: total_g + new_g, acc, grad_weights)
        return (acc, (result.astype(jnp.bfloat16), grad_hidden))
    start_acc = jax.tree.map(jnp.zeros_like, weights)
    totals, (outs_seq, grads_seq) = lax.scan(one_sequence, start_acc, (inputs, cotangents, seg_rows, pos_rows))
    return (outs_seq.reshape(TOKENS, D), grads_seq.reshape(TOKENS, D), totals[0], totals[1], totals[2], totals[3], totals[4], totals[5], totals[6], totals[7])
```

```python
import jax
import jax.numpy as jnp
from jax import lax
from jax.sharding import Mesh, PartitionSpec as P

HEAD_DIM = 128
EPS = 1e-06
THETA = 500000.0
NEG = -1e30
F32 = jnp.float32
BF16 = jnp.bfloat16


def dot_rows_cols(left, right):
    return jnp.dot(left, right, preferred_element_type=F32)


def contract_cols(left, right):
    return lax.dot_general(left, right, (((1,), (1,)), ((), ())), preferred_element_type=F32)


def contract_rows(left, right):
    return lax.dot_general(left, right, (((0,), (0,)), ((), ())), preferred_element_type=F32)


def swap(values, axis):
    return lax.ppermute(values, axis, [(0, 1), (1, 0)])


def pick(flag, yes, no):
    return jnp.where(flag, yes, no)


class Layout:
    def __init__(self, n_dp, n_tensor):
        self.dp_axes = tuple(f"d{i}" for i in range(n_dp.bit_length() - 1))
        self.tensor_axes = tuple(f"t{i}" for i in range(n_tensor.bit_length() - 1))
        self.col_axis = self.dp_axes[1]
        self.row_axes = tuple(a for a in self.dp_axes if a != self.col_axis)
        self.core, self.side = self.tensor_axes[1], self.tensor_axes[0]
        self.n_dp = n_dp
        self.n_bits = len(self.dp_axes)

    def shape_of(self):
        return (2,) * (len(self.dp_axes) + len(self.tensor_axes))

    def dp_mask(self, axis):
        return 1 << (self.n_bits - 1 - self.dp_axes.index(axis))

    def block_order(self):
        order = []
        for j in range(1 << len(self.row_axes)):
            block = 0
            for i, axis in enumerate(self.row_axes):
                if (j >> i) & 1:
                    block |= self.dp_mask(axis)
            order += [block, block | self.dp_mask(self.col_axis)]
        return order

    def flip_blocks(self, blocks):
        for axis in self.row_axes:
            flag, mask = lax.axis_index(axis) == 1, self.dp_mask(axis)
            blocks = [pick(flag, blocks[b ^ mask], blocks[b]) for b in range(len(blocks))]
        return blocks

    def to_relative(self, values):
        width = values.shape[-1] // self.n_dp
        blocks = [values[..., b * width : (b + 1) * width] for b in range(self.n_dp)]
        blocks = self.flip_blocks(blocks)
        return jnp.concatenate([blocks[b] for b in self.block_order()], -1)

    def from_relative(self, values):
        width = values.shape[-1] // self.n_dp
        blocks = [None] * self.n_dp
        for place, b in enumerate(self.block_order()):
            blocks[b] = values[..., place * width : (place + 1) * width]
        return jnp.concatenate(self.flip_blocks(blocks), -1)


def rope_tables(pos_row):
    half_dim = HEAD_DIM // 2
    inverse = THETA ** (-(jnp.arange(half_dim, dtype=F32) * 2.0 / HEAD_DIM))
    angles = pos_row.astype(F32)[..., None] * inverse
    return jnp.cos(angles)[..., None, :], jnp.sin(angles)[..., None, :]


def rotate(values, cos_tab, sin_tab):
    half_dim = values.shape[-1] // 2
    first, second = values[..., :half_dim], values[..., half_dim:]
    return jnp.concatenate(
        [first * cos_tab - second * sin_tab, second * cos_tab + first * sin_tab], -1
    )


def unrotate(values, cos_tab, sin_tab):
    half_dim = values.shape[-1] // 2
    first, second = values[..., :half_dim], values[..., half_dim:]
    return jnp.concatenate(
        [first * cos_tab + second * sin_tab, second * cos_tab - first * sin_tab], -1
    )


def block_program(lay):
    col, side, core = lay.col_axis, lay.side, lay.core

    def my(axis):
        return lax.axis_index(axis)

    def halve_columns(weight):
        half = weight.shape[1] // 2
        low, high = weight[:, :half], weight[:, half:]
        first = my(col) == 0
        got = swap(pick(first, high, low), col)
        mine = pick(first, low, high)
        return jnp.concatenate([pick(first, mine, got), pick(first, got, mine)], 0)

    def gather_rows(block):
        pieces = [block]
        for axis in lay.row_axes:
            pieces = pieces + [swap(piece, axis) for piece in pieces]
        return pieces

    def scatter_rows(pieces):
        for axis in reversed(lay.row_axes):
            half = len(pieces) // 2
            received = [swap(piece.astype(BF16), axis) for piece in pieces[half:]]
            pieces = [a.astype(F32) + b.astype(F32) for a, b in zip(pieces[:half], received)]
        (total,) = pieces
        half = total.shape[0] // 2
        top, bottom = total[:half], total[half:]
        first = my(col) == 0
        got = swap(pick(first, bottom, top).astype(BF16), col).astype(F32)
        mine = pick(first, top, bottom)
        return pick(first, mine, got), pick(first, got, mine)

    def gather_tokens(own):
        half = own.shape[0] // 2
        a0, b0 = own[:half], own[half:]
        a_side, b_col = swap(a0, side), swap(b0, col)
        a_col, a_both = swap(a0, col), swap(a_side, col)
        b_side, b_both = swap(b0, side), swap(b_col, side)
        mine = jnp.concatenate([a0, b0, a_side, b_side, a_col, b_col, a_both, b_both], 0)
        return jnp.concatenate([mine, swap(mine, core)], 0)

    def scatter_tokens(part):
        n = part.shape[0] // 2
        part = part[:n] + swap(part[n:].astype(BF16), core).astype(F32)
        half = n // 8
        a0, b0, a_side, b_side, a_col, b_col, a_both, b_both = (
            part[i * half : (i + 1) * half] for i in range(8)
        )

        def add(own, other, axis):
            return own + swap(other.astype(BF16), axis).astype(F32)

        a1 = add(a_side, a_both, col)
        a0 = add(a0, a_col, col)
        b1 = add(b_col, b_both, side)
        b0 = add(b0, b_side, side)
        return jnp.concatenate([add(a0, a1, side), add(b0, b1, col)], 0)

    def token_rows(values):
        quarters = values.reshape(4, -1)
        rows = [quarters[0:1], quarters[1:2], quarters[2:3], quarters[3:4]]
        for axis, mask in ((side, 2), (core, 1)):
            flag = my(axis) == 1
            rows = [pick(flag, rows[i ^ mask], rows[i]) for i in range(4)]
        own = jnp.concatenate(rows, 0)
        other = swap(own, col)
        order = [own[0:1], own[2:3], other[0:1], other[2:3], own[1:2], own[3:4], other[1:2], other[3:4]]
        return jnp.concatenate(order, 0)

    def add_all(values, axes):
        for axis in axes:
            values = values + swap(values, axis)
        return values

    def add_stats(rows):
        rows = rows.reshape(-1, 2, 2, 2, rows.shape[1] // 8)
        for dim, axis in ((1, core), (2, col), (3, side)):
            rows = rows + jnp.flip(swap(rows, axis), dim)
        return rows.reshape(rows.shape[0], -1)

    def on_device(
        hidden_in, out_grad, w_query, w_key, w_value, w_out, w_gate, w_up, w_down, gains, seg_ids, positions
    ):
        model_width = hidden_in.shape[1]
        head_cols = w_query.shape[1] // 2
        n_heads = head_cols // HEAD_DIM
        n_tokens = hidden_in.shape[0] * 8
        seq_len = n_tokens // 2
        score_scale = HEAD_DIM ** (-0.5)
        place = my(side) * 4 + my(core) * 2 + my(col)
        offset = place * head_cols
        gain_query = lax.dynamic_slice_in_dim(gains[0], offset, head_cols)
        gain_key = lax.dynamic_slice_in_dim(gains[1], offset, head_cols)
        gain_post = lay.to_relative(gains[2:4])
        gain_attn, gain_mlp = gain_post[0:1], gain_post[1:2]

        x_low = lay.to_relative(hidden_in)
        grad_out = lay.to_relative(out_grad).astype(F32)
        x_all = gather_tokens(x_low)

        qkv_pieces = gather_rows(
            jnp.concatenate([halve_columns(w) for w in (w_query, w_key, w_value)], 1)
        )
        out_pieces = gather_rows(halve_columns(w_out))
        gate_pieces = gather_rows(halve_columns(w_gate))
        up_pieces = gather_rows(halve_columns(w_up))
        down_pieces = gather_rows(halve_columns(w_down))
        n_pieces = len(qkv_pieces)
        piece = model_width // n_pieces
        qkv_w = jnp.concatenate(qkv_pieces, 0)
        out_w = jnp.concatenate(out_pieces, 0)
        gate_w = jnp.concatenate(gate_pieces, 0)
        up_w = jnp.concatenate(up_pieces, 0)
        down_w = jnp.concatenate(down_pieces, 0)

        pos_rows = token_rows(positions)
        seg_rows = token_rows(seg_ids)
        ids_rows = token_rows(jnp.arange(seq_len, dtype=jnp.int32))
        per = seq_len // 4

        def by_seq(rows):
            return rows.reshape(2, 2, 2 * per).transpose(1, 0, 2).reshape(2, seq_len)

        def heads_of(values):
            return (
                values.reshape(2, 2, 2 * per, n_heads, HEAD_DIM)
                .transpose(1, 0, 2, 3, 4)
                .reshape(2, seq_len, n_heads, HEAD_DIM)
            )

        def tokens_of(values):
            return (
                values.reshape(2, 2, 2 * per, n_heads, HEAD_DIM)
                .transpose(1, 0, 2, 3, 4)
                .reshape(n_tokens, head_cols)
            )

        seg_seq, ids_seq = by_seq(seg_rows), by_seq(ids_rows)
        cos_tab, sin_tab = rope_tables(by_seq(pos_rows))
        mask = (seg_seq[:, :, None] == seg_seq[:, None, :]) & (ids_seq[:, :, None] >= ids_seq[:, None, :])

        qkv = dot_rows_cols(x_all, qkv_w)
        queries, key_proj = qkv[:, :head_cols], qkv[:, head_cols : 2 * head_cols]
        value_low = heads_of(qkv[:, 2 * head_cols :].astype(BF16))
        squares = add_stats(
            jnp.stack([jnp.sum(queries * queries, -1), jnp.sum(key_proj * key_proj, -1)], 0)
        )
        norm_query = lax.rsqrt(squares[0] / model_width + EPS)[:, None]
        norm_key = lax.rsqrt(squares[1] / model_width + EPS)[:, None]
        query_hat = queries * norm_query
        key_hat = key_proj * norm_key
        q_rot = rotate(heads_of(query_hat * gain_query), cos_tab, sin_tab).astype(BF16)
        k_rot = rotate(heads_of(key_hat * gain_key), cos_tab, sin_tab).astype(BF16)
        scores = jnp.einsum("bqhd,bkhd->bhqk", q_rot, k_rot, preferred_element_type=F32) * score_scale
        scores = jnp.where(mask[:, None], scores, NEG)
        row_max = jnp.max(scores, -1, keepdims=True)
        exp_scores = jnp.exp(scores - row_max)
        row_total = jnp.sum(exp_scores, -1, keepdims=True)
        prob_full = exp_scores / row_total
        prob_low = prob_full.astype(BF16)
        attn_low = tokens_of(
            jnp.einsum("bhqk,bkhd->bqhd", prob_low, value_low, preferred_element_type=F32).astype(BF16)
        )
        attn_sum = scatter_tokens(contract_cols(attn_low, out_w))
        norm_attn = lax.rsqrt(jnp.mean(attn_sum * attn_sum, -1, keepdims=True) + EPS)
        attn_hat = attn_sum * norm_attn
        resid = x_low.astype(F32) + attn_hat * gain_attn

        mlp_in = gather_tokens(resid.astype(BF16))
        gate_proj = dot_rows_cols(mlp_in, gate_w)
        up_proj = dot_rows_cols(mlp_in, up_w)
        sig_gate = jax.nn.sigmoid(gate_proj)
        act_gate = gate_proj * sig_gate
        hidden_act = (act_gate * up_proj).astype(BF16)
        mlp_sum = jnp.concatenate(
            [scatter_tokens(contract_cols(hidden_act, piece_w)) for piece_w in down_pieces], 1
        )
        norm_mlp = lax.rsqrt(jnp.mean(mlp_sum * mlp_sum, -1, keepdims=True) + EPS)
        mlp_hat = mlp_sum * norm_mlp
        hidden_out = lay.from_relative((resid + mlp_hat * gain_mlp).astype(BF16))

        gain_row_mlp = jnp.sum(grad_out * mlp_hat, 0, keepdims=True)
        scaled = grad_out * gain_mlp
        grad_mlp = norm_mlp * (scaled - mlp_hat * jnp.mean(mlp_hat * scaled, -1, keepdims=True))
        grad_mlp_all = gather_tokens(grad_mlp.astype(BF16))

        def weight_grad(left, right):
            return [
                contract_rows(left[:, i * piece : (i + 1) * piece], right).astype(BF16) for i in range(n_pieces)
            ]

        down_out = scatter_rows(weight_grad(grad_mlp_all, hidden_act))
        grad_act = dot_rows_cols(grad_mlp_all, down_w)
        grad_gate = (grad_act * up_proj * (sig_gate * (1.0 + gate_proj * (1.0 - sig_gate)))).astype(BF16)
        grad_up = (grad_act * act_gate).astype(BF16)
        grad_resid = grad_out + scatter_tokens(contract_cols(grad_gate, gate_w) + contract_cols(grad_up, up_w))
        gate_out = scatter_rows(weight_grad(mlp_in, grad_gate))
        up_out = scatter_rows(weight_grad(mlp_in, grad_up))

        gain_row_attn = jnp.sum(grad_resid * attn_hat, 0, keepdims=True)
        scaled = grad_resid * gain_attn
        grad_attn = norm_attn * (scaled - attn_hat * jnp.mean(attn_hat * scaled, -1, keepdims=True))
        grad_attn_all = gather_tokens(grad_attn.astype(BF16))
        grad_heads = heads_of(dot_rows_cols(grad_attn_all, out_w).astype(BF16))
        out_grad_pieces = weight_grad(grad_attn_all, attn_low)
        grad_prob = jnp.einsum("bqhd,bkhd->bhqk", grad_heads, value_low, preferred_element_type=F32)
        row_dot = jnp.sum(prob_full * grad_prob, -1, keepdims=True)
        grad_scores = (prob_full * (grad_prob - row_dot)).astype(BF16)
        grad_q_rot = jnp.einsum("bhqk,bkhd->bqhd", grad_scores, k_rot, preferred_element_type=F32) * score_scale
        grad_k_rot = jnp.einsum("bhqk,bqhd->bkhd", grad_scores, q_rot, preferred_element_type=F32) * score_scale
        grad_value = jnp.einsum("bhqk,bqhd->bkhd", prob_low, grad_heads, preferred_element_type=F32)
        grad_value_low = tokens_of(grad_value.astype(BF16))
        grad_query_n = tokens_of(unrotate(grad_q_rot, cos_tab, sin_tab))
        grad_key_n = tokens_of(unrotate(grad_k_rot, cos_tab, sin_tab))
        grad_query_hat = grad_query_n * gain_query
        grad_key_hat = grad_key_n * gain_key
        inner = add_stats(
            jnp.stack([jnp.sum(query_hat * grad_query_hat, -1), jnp.sum(key_hat * grad_key_hat, -1)], 0)
        )
        grad_query_low = (norm_query * (grad_query_hat - query_hat * inner[0][:, None] / model_width)).astype(BF16)
        grad_key_low = (norm_key * (grad_key_hat - key_hat * inner[1][:, None] / model_width)).astype(BF16)
        qkv_right = jnp.concatenate([grad_query_low, grad_key_low, grad_value_low], 1)
        in_grad = grad_resid + scatter_tokens(contract_cols(qkv_right, qkv_w))
        qkv_grad_pieces = weight_grad(x_all, qkv_right)
        attn_a, attn_b = scatter_rows(
            [jnp.concatenate([a, b], 1) for a, b in zip(qkv_grad_pieces, out_grad_pieces)]
        )
        attn_outs = [
            jnp.concatenate(
                [attn_a[:, i * head_cols : (i + 1) * head_cols], attn_b[:, i * head_cols : (i + 1) * head_cols]], 1
            )
            for i in range(4)
        ]

        head_gains = jnp.stack([jnp.sum(grad_query_n * query_hat, 0), jnp.sum(grad_key_n * key_hat, 0)])
        head_rows = lax.dynamic_update_slice(jnp.zeros((2, model_width), F32), head_gains, (jnp.int32(0), offset))
        post_rows = lay.from_relative(jnp.concatenate([gain_row_attn, gain_row_mlp], 0))
        gains_grad = add_all(
            jnp.concatenate([head_rows, post_rows], 0), lay.tensor_axes[::-1] + lay.dp_axes[::-1]
        )
        return (
            hidden_out,
            lay.from_relative(in_grad),
            attn_outs[0],
            attn_outs[1],
            attn_outs[2],
            attn_outs[3],
            jnp.concatenate(gate_out, 1),
            jnp.concatenate(up_out, 1),
            jnp.concatenate(down_out, 1),
            gains_grad,
        )

    return on_device


def solution(mesh):
    lay = Layout(mesh.shape["dp"], mesh.shape["tensor"])
    fine = Mesh(mesh.devices.reshape(lay.shape_of()), lay.dp_axes + lay.tensor_axes)
    tokens = P(lay.dp_axes + lay.tensor_axes, None)
    weights = P(lay.dp_axes, lay.tensor_axes)
    rows = P(lay.dp_axes)
    return jax.shard_map(
        block_program(lay),
        mesh=fine,
        in_specs=(tokens, tokens) + (weights,) * 7 + (P(), rows, rows),
        out_specs=(tokens, tokens) + (weights,) * 7 + (P(),),
        check_vma=False,
    )
```

```python
import jax
import jax.numpy as jnp
from jax import lax
from jax.experimental import pallas as pl
from jax.experimental.pallas import tpu as pltpu
from jax.sharding import Mesh, PartitionSpec as P

HEAD_DIM = 128
EPS = 1e-06
THETA = 500000.0
NEG = -1e30
F32 = jnp.float32
BF16 = jnp.bfloat16


def dot_rows_cols(left, right):
    return jnp.dot(left, right, preferred_element_type=F32)


def contract_cols(left, right):
    return lax.dot_general(left, right, (((1,), (1,)), ((), ())), preferred_element_type=F32)


def contract_rows(left, right):
    return lax.dot_general(left, right, (((0,), (0,)), ((), ())), preferred_element_type=F32)


def swap(values, axis):
    return lax.ppermute(values, axis, [(0, 1), (1, 0)])


def pick(flag, yes, no):
    return jnp.where(flag, yes, no)


def after(values, *done):
    return lax.optimization_barrier((values,) + done)[0] if done else values


class Net:
    def send(self, values, axis):
        return swap(values, axis)


def region(flag, step):
    out = jax.eval_shape(step)
    return lax.cond(flag, step, lambda: jax.tree.map(lambda leaf: jnp.zeros(leaf.shape, leaf.dtype), out))


def meet(*values):
    leaves, tree = jax.tree.flatten(values)
    return jax.tree.unflatten(tree, lax.optimization_barrier(tuple(leaves)))


class Sequence:
    def __init__(self):
        self.done = ()

    def wait(self, *received):
        self.done = self.done + received

    def run(self, step, *operands):
        if self.done:
            operands = lax.optimization_barrier(operands + self.done)[: len(operands)]
        out = step(*operands)
        self.done = out if isinstance(out, tuple) else (out,)
        return out


class Layout:
    def __init__(self, n_dp, n_tensor):
        self.dp_axes = tuple(f"d{i}" for i in range(n_dp.bit_length() - 1))
        self.tensor_axes = tuple(f"t{i}" for i in range(n_tensor.bit_length() - 1))
        self.col_axis = self.dp_axes[1]
        self.far = self.dp_axes[0]
        self.near = tuple(a for a in self.dp_axes if a not in (self.far, self.col_axis))
        self.core, self.side = self.tensor_axes[1], self.tensor_axes[0]
        self.n_dp = n_dp
        self.n_bits = len(self.dp_axes)

    def shape_of(self):
        return (2,) * (len(self.dp_axes) + len(self.tensor_axes))

    def dp_mask(self, axis):
        return 1 << (self.n_bits - 1 - self.dp_axes.index(axis))

    def block_order(self):
        order = []
        for j in range(1 << len(self.near)):
            block = sum(self.dp_mask(axis) for i, axis in enumerate(self.near) if (j >> i) & 1)
            for ahead in (0, self.dp_mask(self.far)):
                order += [block | ahead, block | ahead | self.dp_mask(self.col_axis)]
        return order

    def flip_blocks(self, blocks):
        for axis in self.near:
            flag, mask = lax.axis_index(axis) == 1, self.dp_mask(axis)
            blocks = [pick(flag, blocks[b ^ mask], blocks[b]) for b in range(len(blocks))]
        return blocks

    def to_relative(self, values):
        width = values.shape[-1] // self.n_dp
        blocks = [values[..., b * width : (b + 1) * width] for b in range(self.n_dp)]
        blocks = self.flip_blocks(blocks)
        return jnp.concatenate([blocks[b] for b in self.block_order()], -1)

    def from_relative(self, values):
        width = values.shape[-1] // self.n_dp
        blocks = [None] * self.n_dp
        for place, b in enumerate(self.block_order()):
            blocks[b] = values[..., place * width : (place + 1) * width]
        return jnp.concatenate(self.flip_blocks(blocks), -1)


def rope_tables(pos_col):
    lane = jnp.arange(HEAD_DIM, dtype=jnp.int32)[None, :]
    pair = (lane % (HEAD_DIM // 2)).astype(F32)
    inverse = THETA ** (-(pair * 2.0 / HEAD_DIM))
    angles = pos_col.astype(F32) * inverse
    return jnp.cos(angles), jnp.sin(angles) * jnp.where(lane < HEAD_DIM // 2, -1.0, 1.0)


def load_rows(ref):
    values = ref[...]
    return values.reshape(-1, values.shape[-1])


def head_scores(q_ref, k_ref, norm_ref, gain_q_ref, gain_k_ref, cos_ref, sin_ref, mask_ref):
    norms, cos_tab, sin_tab = load_rows(norm_ref), load_rows(cos_ref), load_rows(sin_ref)

    def rotated(values, gain):
        values = values * gain
        return (values * cos_tab + pltpu.roll(values, HEAD_DIM // 2, 1) * sin_tab).astype(BF16)

    query_hat = load_rows(q_ref) * norms[:, 0:1]
    key_hat = load_rows(k_ref) * norms[:, 1:2]
    q_rot = rotated(query_hat, gain_q_ref[...])
    k_rot = rotated(key_hat, gain_k_ref[...])
    scores = contract_cols(q_rot, k_rot) * HEAD_DIM ** (-0.5)
    scores = jnp.where(mask_ref[0] > 0, scores, NEG)
    exp_scores = jnp.exp(scores - jnp.max(scores, -1, keepdims=True))
    probs = exp_scores / jnp.sum(exp_scores, -1, keepdims=True)
    return query_hat, key_hat, q_rot, k_rot, probs, cos_tab, sin_tab


def attend_kernel(q_ref, k_ref, v_ref, norm_ref, gain_q_ref, gain_k_ref, cos_ref, sin_ref, mask_ref, out_ref):
    probs = head_scores(q_ref, k_ref, norm_ref, gain_q_ref, gain_k_ref, cos_ref, sin_ref, mask_ref)[4]
    out = dot_rows_cols(probs.astype(BF16), load_rows(v_ref).astype(BF16)).astype(BF16)
    out_ref[...] = out.reshape(out_ref.shape)


def attend_back_kernel(
    q_ref, k_ref, v_ref, norm_ref, gain_q_ref, gain_k_ref, cos_ref, sin_ref, mask_ref, grad_ref,
    grad_q_ref, grad_k_ref, grad_v_ref, inner_ref, gains_ref,
):
    query_hat, key_hat, q_rot, k_rot, probs, cos_tab, sin_tab = head_scores(
        q_ref, k_ref, norm_ref, gain_q_ref, gain_k_ref, cos_ref, sin_ref, mask_ref
    )
    grad_head = load_rows(grad_ref)
    grad_prob = contract_cols(grad_head, load_rows(v_ref).astype(BF16))
    row_dot = jnp.sum(probs * grad_prob, -1, keepdims=True)
    grad_scores = (probs * (grad_prob - row_dot)).astype(BF16)
    scale = HEAD_DIM ** (-0.5)

    def unrotated(values):
        return values * cos_tab - pltpu.roll(values, HEAD_DIM // 2, 1) * sin_tab

    grad_q = unrotated(dot_rows_cols(grad_scores, k_rot) * scale)
    grad_k = unrotated(contract_rows(grad_scores, q_rot) * scale)
    grad_v = contract_rows(probs.astype(BF16), grad_head).astype(BF16)
    product_q, product_k = grad_q * query_hat, grad_k * key_hat
    inner_q = jnp.sum(product_q * gain_q_ref[...], -1, keepdims=True)
    inner_k = jnp.sum(product_k * gain_k_ref[...], -1, keepdims=True)
    grad_q_ref[...] = grad_q.reshape(grad_q_ref.shape)
    grad_k_ref[...] = grad_k.reshape(grad_k_ref.shape)
    grad_v_ref[...] = grad_v.reshape(grad_v_ref.shape)
    inner_ref[...] = jnp.concatenate([inner_q, inner_k], 1).reshape(inner_ref.shape)
    gains_ref[...] = jnp.concatenate(
        [jnp.sum(product_q, 0, keepdims=True), jnp.sum(product_k, 0, keepdims=True)], 0
    ).reshape(gains_ref.shape)


def attention(qkv, norms, gain_query, gain_key, cos_tab, sin_tab, mask, grad_heads=None):
    n_tokens = qkv.shape[0]
    rows, n_heads = n_tokens // 4, qkv.shape[1] // (3 * HEAD_DIM)

    def split(values):
        return values.reshape(2, 2, rows, values.shape[-1])

    def columns(first):
        return pl.BlockSpec((2, 1, rows, HEAD_DIM), lambda s, h: (0, s, 0, first + h))

    def whole(width):
        return pl.BlockSpec((2, 1, rows, width), lambda s, h: (0, s, 0, 0))

    gain = pl.BlockSpec((1, HEAD_DIM), lambda s, h: (0, h))
    in_specs = [columns(0), columns(n_heads), columns(2 * n_heads), whole(2), gain, gain, whole(HEAD_DIM), whole(HEAD_DIM)]
    in_specs.append(pl.BlockSpec((1, 2 * rows, 2 * rows), lambda s, h: (s, 0, 0)))
    heads = split(qkv)
    operands = [heads, heads, heads, split(norms), gain_query[None], gain_key[None], split(cos_tab), split(sin_tab), mask]
    shape = (2, 2, rows, n_heads * HEAD_DIM)
    kernel, out_specs, out_shape = attend_kernel, columns(0), jax.ShapeDtypeStruct(shape, BF16)
    if grad_heads is not None:
        in_specs.append(columns(0))
        operands.append(split(grad_heads))
        kernel = attend_back_kernel
        out_specs = (
            columns(0),
            columns(0),
            columns(0),
            pl.BlockSpec((1, 2, 1, rows, 2), lambda s, h: (h, 0, s, 0, 0)),
            pl.BlockSpec((1, 2, HEAD_DIM), lambda s, h: (s, 0, h)),
        )
        out_shape = (
            jax.ShapeDtypeStruct(shape, F32),
            jax.ShapeDtypeStruct(shape, F32),
            jax.ShapeDtypeStruct(shape, BF16),
            jax.ShapeDtypeStruct((n_heads, 2, 2, rows, 2), F32),
            jax.ShapeDtypeStruct((2, 2, n_heads * HEAD_DIM), F32),
        )
    out = pl.pallas_call(
        kernel,
        grid=(2, n_heads),
        in_specs=in_specs,
        out_specs=out_specs,
        out_shape=out_shape,
        compiler_params=pltpu.CompilerParams(vmem_limit_bytes=48 * 1024 * 1024),
        cost_estimate=pl.CostEstimate(flops=1 << 30, bytes_accessed=1 << 23, transcendentals=1 << 20),
    )(*operands)
    if grad_heads is None:
        return out.reshape(n_tokens, -1)
    return tuple(part.reshape(n_tokens, -1) for part in out[:3]) + (out[3], jnp.sum(out[4], 0))


def block_program(lay):
    col, side, core = lay.col_axis, lay.side, lay.core

    def my(axis):
        return lax.axis_index(axis)

    def halves(weights):
        half = [w.shape[1] // 2 for w in weights]
        low = jnp.concatenate([w[:, :h] for w, h in zip(weights, half)], 1)
        high = jnp.concatenate([w[:, h:] for w, h in zip(weights, half)], 1)
        return low, high

    def leaving(weights):
        low, high = halves(weights)
        return pick(my(col) == 0, high, low)

    def both_rows(weights, got):
        low, high = halves(weights)
        first = my(col) == 0
        return jnp.concatenate([pick(first, low, got), pick(first, got, high)], 0)

    def ahead(block):
        return lax.all_gather(block, lay.far, axis=0, tiled=True)

    def beyond(both):
        half = both.shape[0] // 2
        return lax.dynamic_slice_in_dim(both, (1 - my(lay.far)) * half, half, 0)

    def in_two(own, other):
        first = my(lay.far) == 0
        return jnp.concatenate([pick(first, own, other), pick(first, other, own)], 0)

    def behind(total):
        return lax.psum_scatter(total.astype(BF16), lay.far, scatter_dimension=0, tiled=True)

    def spread(net, block):
        pieces = [block]
        for axis in lay.near:
            pieces = pieces + [net.send(piece, axis) for piece in pieces]
        return pieces

    def begin(net, grads):
        return [net.send(grad, lay.near[-1]) for grad in grads]

    def finish(net, keeps, received):
        pieces = [a.astype(F32) + b.astype(F32) for a, b in zip(keeps, received)]
        for axis in reversed(lay.near[:-1]):
            half = len(pieces) // 2
            others = [net.send(piece.astype(BF16), axis) for piece in pieces[half:]]
            pieces = [a + b.astype(F32) for a, b in zip(pieces[:half], others)]
        return pieces[0].astype(BF16)

    def to_leave(total):
        half = total.shape[0] // 2
        return pick(my(col) == 0, total[half:], total[:half]).astype(BF16)

    def owned(total, got):
        half = total.shape[0] // 2
        first = my(col) == 0
        mine, got = pick(first, total[:half], total[half:]), got.astype(F32)
        return pick(first, mine, got), pick(first, got, mine)

    def gather_begin(net, own):
        half = own.shape[0] // 2
        a0, b0 = own[:half], own[half:]
        return a0, b0, net.send(a0, side), net.send(b0, col)

    def gather_middle(net, state):
        a0, b0, a_side, b_col = state
        half = a0.shape[0]
        a_far = net.send(jnp.concatenate([a0, a_side], 0), col)
        b_far = net.send(jnp.concatenate([b0, b_col], 0), side)
        return [a0, b0, a_side, b_far[:half], a_far[:half], b_col, a_far[half:], b_far[half:]], (a_far, b_far)

    def gather_end(net, state):
        mine = jnp.concatenate(state[0], 0)
        other = net.send(mine, core)
        return jnp.concatenate([mine, other], 0), other

    def scatter_begin(net, part):
        n = part.shape[0] // 2
        return part[:n], net.send(part[n:].astype(BF16), core)

    def scatter_second(net, state):
        part = state[0] + state[1].astype(F32)
        half = part.shape[0] // 8
        a0, b0, a_side, b_side, a_col, b_col, a_both, b_both = (part[i * half : (i + 1) * half] for i in range(8))
        received = (
            net.send(jnp.concatenate([a_col, a_both], 0).astype(BF16), col),
            net.send(jnp.concatenate([b_side, b_both], 0).astype(BF16), side),
        )
        return jnp.concatenate([a0, a_side], 0), jnp.concatenate([b0, b_col], 0), received

    def scatter_third(net, state):
        a_sum, b_sum = (own + got.astype(F32) for own, got in zip(state[:2], state[2]))
        half = a_sum.shape[0] // 2
        received = net.send(a_sum[half:].astype(BF16), side), net.send(b_sum[half:].astype(BF16), col)
        return a_sum[:half], b_sum[:half], received

    def scatter_end(state):
        a0, b0, received = state
        return jnp.concatenate([a0 + received[0].astype(F32), b0 + received[1].astype(F32)], 0)

    def token_rows(values, exchange):
        quarters = values.reshape(4, -1)
        rows = [quarters[0:1], quarters[1:2], quarters[2:3], quarters[3:4]]
        for axis, mask in ((side, 2), (core, 1)):
            flag = my(axis) == 1
            rows = [pick(flag, rows[i ^ mask], rows[i]) for i in range(4)]
        own = jnp.concatenate(rows, 0)
        other = exchange(own)
        order = [own[0:1], own[2:3], other[0:1], other[2:3], own[1:2], own[3:4], other[1:2], other[3:4]]
        return jnp.concatenate(order, 0)

    def token_rows_of(positions, seg_ids, net):
        rows = []

        def exchange(own):
            rows.append(own)
            return own

        token_rows(positions, exchange)
        token_rows(seg_ids, exchange)
        other = net.send(jnp.concatenate(rows, 0), col)
        return [
            token_rows(values, lambda own, i=i: other[4 * i : 4 * i + 4])
            for i, values in enumerate((positions, seg_ids))
        ]

    def add_all(net, values, axes):
        for axis in axes:
            received = net.send(values, axis)
            values = values + received
        return values

    def add_stats(net, rows):
        rows = rows.reshape(-1, 2, 2, 2, rows.shape[1] // 8)
        for dim, axis in ((1, core), (2, col), (3, side)):
            received = net.send(rows, axis)
            rows = rows + jnp.flip(received, dim)
        return rows.reshape(rows.shape[0], -1), received

    def on_device(
        hidden_in, out_grad, w_query, w_key, w_value, w_out, w_gate, w_up, w_down, gains, seg_ids, positions
    ):
        model_width = hidden_in.shape[1]
        head_cols = w_query.shape[1] // 2
        n_heads = head_cols // HEAD_DIM
        n_tokens = hidden_in.shape[0] * 8
        seq_len = n_tokens // 2
        score_scale = HEAD_DIM ** (-0.5)
        place = my(side) * 4 + my(core) * 2 + my(col)
        offset = place * head_cols
        per = seq_len // 4

        def by_seq(rows):
            return rows.reshape(2, 2, 2 * per).transpose(1, 0, 2).reshape(2, seq_len)

        net = Net()
        flag = positions[0] >= 0
        n_near = 1 << len(lay.near)
        piece = model_width // n_near
        kept_pieces, sent_pieces = range(n_near // 2), range(n_near // 2, n_near)

        def stack(*parts):
            return jnp.concatenate(parts, 0)

        def by_rows(left, pieces, cols=slice(None)):
            return sum(
                dot_rows_cols(left[:, j * piece : (j + 1) * piece], block[:, cols]) for j, block in enumerate(pieces)
            )

        def weight_grad(seq, left, right, which):
            return [
                seq.run(
                    lambda a, b: contract_rows(a, b).astype(BF16), left[:, j * piece : (j + 1) * piece], right
                )
                for j in which
            ]

        attn_weights = [w_query, w_key, w_value, w_out]

        def part_first():
            block_attn = both_rows(attn_weights, net.send(leaving(attn_weights), col))
            pos_rows, seg_rows = token_rows_of(positions, seg_ids, net)
            return block_attn, leaving([w_gate]), leaving([w_up]), pos_rows, seg_rows, lay.to_relative(hidden_in)

        block_attn, leave_gate, leave_up, pos_rows, seg_rows, x_low = region(flag, part_first)
        far_attn, own_attn = ahead(block_attn), spread(net, block_attn)[1:]

        def part_tokens():
            state = gather_middle(net, gather_begin(net, x_low))
            got_gate = net.send(after(leave_gate, *state[1]), col)
            x_all, other = gather_end(net, state)
            return x_all, leaving([w_down]), both_rows([w_gate], got_gate)

        out = region(flag, part_tokens)
        far_attn, own_attn, (x_all, leave_down, block_gate) = meet(far_attn, own_attn, out)
        relay_attn = spread(net, beyond(far_attn))[1:]
        far_gate, got_up = ahead(block_gate), net.send(leave_up, col)

        def part_tables():
            cos_tab, sin_tab = rope_tables(pos_rows.reshape(n_tokens, 1))
            ids_rows = token_rows(jnp.arange(seq_len, dtype=jnp.int32), lambda rows: rows)
            seg_seq, ids_seq = by_seq(seg_rows), by_seq(ids_rows)
            mask = (seg_seq[:, :, None] == seg_seq[:, None, :]) & (ids_seq[:, :, None] >= ids_seq[:, None, :])
            mask = mask.astype(F32)
            gain_query = lax.dynamic_slice_in_dim(gains[0], offset, head_cols)
            gain_key = lax.dynamic_slice_in_dim(gains[1], offset, head_cols)
            gain_post = lay.to_relative(gains[2:4])
            more = gain_query, gain_key, gain_post[0:1], gain_post[1:2], lay.to_relative(out_grad).astype(F32)
            return cos_tab, sin_tab, mask, more

        out = region(flag, part_tables)
        relay_attn, got_up, (cos_tab, sin_tab, mask, more) = meet(relay_attn, got_up, out)
        gain_query, gain_key, gain_attn, gain_mlp, grad_out = more
        block_up = both_rows([w_up], got_up)
        far_up, own_up = ahead(block_up), spread(net, block_up)[1:]
        qkv_cols, out_cols = slice(3 * head_cols), slice(3 * head_cols, None)


        def part_qkv():
            near_attn = [far_attn, *(in_two(own, other) for own, other in zip(own_attn, relay_attn))]
            qkv = by_rows(x_all, near_attn, qkv_cols)
            squares, _ = add_stats(
                net,
                jnp.stack(
                    [jnp.sum(part * part, -1) for part in (qkv[:, :head_cols], qkv[:, head_cols : 2 * head_cols])], 0
                ),
            )
            return near_attn, qkv, squares

        out = region(flag, part_qkv)
        leave_down, (near_attn, qkv, squares) = meet(leave_down, out)
        got_down = net.send(leave_down, col)

        def part_attend():
            norms = lax.rsqrt(squares / model_width + EPS).T
            attn_low = attention(qkv, norms, gain_query, gain_key, cos_tab, sin_tab, mask)
            out_w = stack(*(block[:, out_cols] for block in near_attn))
            state = scatter_begin(net, contract_cols(attn_low, out_w))
            return attn_low, norms, out_w, state

        out = region(flag, part_attend)
        own_up, far_gate, got_down, (attn_low, norms, out_w, state) = meet(own_up, far_gate, got_down, out)
        near_gate = spread(net, far_gate)
        block_down = both_rows([w_down], got_down)
        far_down = ahead(block_down)

        def part_resid():
            attn_sum = scatter_end(scatter_third(net, scatter_second(net, state)))
            norm_attn = lax.rsqrt(jnp.mean(attn_sum * attn_sum, -1, keepdims=True) + EPS)
            attn_hat = attn_sum * norm_attn
            resid = x_low.astype(F32) + attn_hat * gain_attn
            return norm_attn, attn_hat, resid, gather_begin(net, resid.astype(BF16))

        out = region(flag, part_resid)
        near_gate, far_up, (norm_attn, attn_hat, resid, state) = meet(near_gate, far_up, out)
        relay_up = spread(net, beyond(far_up))[1:]
        own_down = spread(net, block_down)[1:]

        def part_gate():
            mlp_in, _ = gather_end(net, gather_middle(net, state))
            return mlp_in, by_rows(mlp_in, near_gate)

        out = region(flag, part_gate)
        relay_up, own_down, far_down, (mlp_in, gate_proj) = meet(relay_up, own_down, far_down, out)
        relay_down = spread(net, beyond(far_down))[1:]

        def part_up():
            near_up = [far_up, *(in_two(own, other) for own, other in zip(own_up, relay_up))]
            up_proj = by_rows(mlp_in, near_up)
            hidden_act = (gate_proj * jax.nn.sigmoid(gate_proj) * up_proj).astype(BF16)
            return up_proj, hidden_act, stack(*near_gate), stack(*near_up)

        out = region(flag, part_up)
        relay_down, (up_proj, hidden_act, gate_w, up_w) = meet(relay_down, out)

        act_halves = slice(hidden_act.shape[1] // 2), slice(hidden_act.shape[1] // 2, None)

        def part_down():
            down_w = stack(far_down, *(in_two(own, other) for own, other in zip(own_down, relay_down)))
            state = scatter_begin(net, contract_cols(hidden_act, down_w))
            mlp_sum = scatter_end(scatter_third(net, scatter_second(net, state)))
            norm_mlp = lax.rsqrt(jnp.mean(mlp_sum * mlp_sum, -1, keepdims=True) + EPS)
            mlp_hat = mlp_sum * norm_mlp
            scaled = grad_out * gain_mlp
            grad_mlp = norm_mlp * (scaled - mlp_hat * jnp.mean(mlp_hat * scaled, -1, keepdims=True))
            grad_mlp_all, _ = gather_end(net, gather_middle(net, gather_begin(net, grad_mlp.astype(BF16))))
            seq = Sequence()
            sends = [weight_grad(seq, grad_mlp_all, hidden_act[:, half], sent_pieces) for half in act_halves]
            return down_w, mlp_hat, grad_mlp_all, sends

        down_w, mlp_hat, grad_mlp_all, sends = region(flag, part_down)
        got_first, got_second = [begin(net, grads) for grads in sends]

        def part_back_act():
            seq = Sequence()
            keeps_first = weight_grad(seq, grad_mlp_all, hidden_act[:, act_halves[0]], kept_pieces)

            def back_act(grad_mlp_all, down_w):
                sig_gate = jax.nn.sigmoid(gate_proj)
                grad_act = dot_rows_cols(grad_mlp_all, down_w)
                grad_gate = (grad_act * up_proj * (sig_gate * (1.0 + gate_proj * (1.0 - sig_gate)))).astype(BF16)
                return grad_gate, (grad_act * (gate_proj * sig_gate)).astype(BF16)

            grad_gate, grad_up = seq.run(back_act, grad_mlp_all, down_w)
            return keeps_first, grad_gate, grad_up, seq.run(contract_cols, grad_gate, gate_w)

        out = region(flag, part_back_act)
        got_first, (keeps_first, grad_gate, grad_up, grad_part) = meet(got_first, out)
        down_first = behind(finish(net, keeps_first, got_first))

        def part_back_resid():
            seq = Sequence()
            state = scatter_begin(net, seq.run(lambda a, b, c: a + contract_cols(b, c), grad_part, grad_up, up_w))
            keeps_second = weight_grad(seq, grad_mlp_all, hidden_act[:, act_halves[1]], kept_pieces)
            return weight_grad(seq, mlp_in, grad_gate, sent_pieces), keeps_second, state

        out = region(flag, part_back_resid)
        got_second, (sends, keeps_second, state) = meet(got_second, out)
        got_gate = begin(net, sends)
        down_second = behind(finish(net, keeps_second, got_second))

        def part_back_attn():
            seq = Sequence()
            later = scatter_second(net, state)
            keeps_gate = weight_grad(seq, mlp_in, grad_gate, kept_pieces)
            seq.wait(*later[2])
            later = scatter_third(net, later)
            sends = weight_grad(seq, mlp_in, grad_up, sent_pieces)
            seq.wait(*later[2])
            grad_resid = grad_out + scatter_end(later)
            scaled = grad_resid * gain_attn
            grad_attn = norm_attn * (scaled - attn_hat * jnp.mean(attn_hat * scaled, -1, keepdims=True))
            first = gather_begin(net, grad_attn.astype(BF16))
            gain_row_attn = jnp.sum(grad_resid * attn_hat, 0, keepdims=True)
            keeps_up = weight_grad(seq, mlp_in, grad_up, kept_pieces)
            return keeps_gate, sends, keeps_up, grad_resid, first, gain_row_attn

        out = region(flag, part_back_attn)
        got_gate, down_first, out = meet(got_gate, down_first, out)
        keeps_gate, sends, keeps_up, grad_resid, state, gain_row_attn = out
        got_up = begin(net, sends)
        total_gate = behind(finish(net, keeps_gate, got_gate))

        def part_back_heads():
            seq = Sequence()
            grad_attn_all, _ = gather_end(net, gather_middle(net, state))
            grad_heads = dot_rows_cols(grad_attn_all, out_w).astype(BF16)
            grads = attention(qkv, norms, gain_query, gain_key, cos_tab, sin_tab, mask, grad_heads)
            sends = [
                jnp.concatenate(pair, 1)
                for pair in zip(
                    weight_grad(seq, x_all, grads[2], sent_pieces), weight_grad(seq, grad_attn_all, attn_low, sent_pieces)
                )
            ]
            return grad_attn_all, grads, sends

        out = region(flag, part_back_heads)
        got_up, down_second, (grad_attn_all, grads, sends) = meet(got_up, down_second, out)
        grad_query_n, grad_key_n, grad_value_low, inner_parts, head_gains = grads
        got_first = begin(net, sends)
        total_up = behind(finish(net, keeps_up, got_up))
        total_down = jnp.concatenate([down_first, down_second], 1)
        got_down = net.send(to_leave(total_down), col)

        def part_back_qkv():
            seq = Sequence()
            inner, received = add_stats(net, jnp.sum(inner_parts, 0).reshape(n_tokens, 2).T)
            keeps_first = [
                jnp.concatenate(pair, 1)
                for pair in zip(
                    weight_grad(seq, x_all, grad_value_low, kept_pieces),
                    weight_grad(seq, grad_attn_all, attn_low, kept_pieces),
                )
            ]
            seq.wait(received)
            inner = inner.T / model_width

            def through_norm(grad, i, gain):
                hat = qkv[:, i * head_cols : (i + 1) * head_cols] * norms[:, i : i + 1]
                return (norms[:, i : i + 1] * (grad * gain - hat * inner[:, i : i + 1])).astype(BF16)

            qk_right = seq.run(
                lambda a, b: jnp.concatenate(
                    [through_norm(a, 0, gain_query), through_norm(b, 1, gain_key)], 1
                ),
                grad_query_n,
                grad_key_n,
            )
            return qk_right, keeps_first, weight_grad(seq, x_all, qk_right, sent_pieces)

        out = region(flag, part_back_qkv)
        got_first, got_down, total_gate, (qk_right, keeps_first, sends) = meet(got_first, got_down, total_gate, out)
        got_second = begin(net, sends)
        vo_total = behind(finish(net, keeps_first, got_first))
        got_gate = net.send(to_leave(total_gate), col)

        def part_in_part():
            keeps_second = weight_grad(Sequence(), x_all, qk_right, kept_pieces)
            qkv_right = jnp.concatenate([qk_right, grad_value_low], 1)
            in_part = jnp.concatenate([contract_cols(qkv_right, part[:, qkv_cols]) for part in near_attn], 1)
            head_rows = lax.dynamic_update_slice(
                jnp.zeros((2, model_width), F32), head_gains, (jnp.int32(0), offset)
            )
            gain_row_mlp = jnp.sum(grad_out * mlp_hat, 0, keepdims=True)
            post_rows = lay.from_relative(jnp.concatenate([gain_row_attn, gain_row_mlp], 0))
            gain_rows = add_all(net, jnp.concatenate([head_rows, post_rows], 0), (side, core))
            return keeps_second, scatter_begin(net, in_part), gain_rows

        out = region(flag, part_in_part)
        got_second, got_gate, total_up, (keeps_second, state, gain_rows) = meet(got_second, got_gate, total_up, out)
        qk_total = behind(finish(net, keeps_second, got_second))

        def part_outputs():
            later = scatter_second(net, state)
            gains_grad = add_all(net, gain_rows, lay.near + (lay.col_axis, lay.far))
            got_up = net.send(to_leave(total_up), col)
            down_grad = jnp.concatenate(owned(total_down, got_down), 1)
            in_grad = lay.from_relative(grad_resid + scatter_end(scatter_third(net, later)))
            hidden_out = lay.from_relative((resid + mlp_hat * gain_mlp).astype(BF16))
            gate_grad = jnp.concatenate(owned(total_gate, got_gate), 1)
            up_grad = jnp.concatenate(owned(total_up, got_up), 1)
            return in_grad, hidden_out, gate_grad, down_grad, up_grad, gains_grad

        out = region(flag, part_outputs)
        vo_total, (in_grad, hidden_out, gate_grad, down_grad, up_grad, gains_grad) = meet(vo_total, out)
        vo_pair = owned(vo_total, net.send(to_leave(vo_total), col))
        qk_pair = owned(qk_total, net.send(to_leave(qk_total), col))
        query_grad, key_grad, value_grad, out_grad_own = (
            jnp.concatenate([part[:, i * head_cols : (i + 1) * head_cols] for part in pair], 1)
            for pair in (qk_pair, vo_pair)
            for i in range(2)
        )
        return (
            hidden_out,
            in_grad,
            query_grad,
            key_grad,
            value_grad,
            out_grad_own,
            gate_grad,
            up_grad,
            down_grad,
            gains_grad,
        )

    return on_device


def solution(mesh):
    lay = Layout(mesh.shape["dp"], mesh.shape["tensor"])
    fine = Mesh(mesh.devices.reshape(lay.shape_of()), lay.dp_axes + lay.tensor_axes)
    tokens = P(lay.dp_axes + lay.tensor_axes, None)
    weights = P(lay.dp_axes, lay.tensor_axes)
    rows = P(lay.dp_axes)
    return jax.shard_map(
        block_program(lay),
        mesh=fine,
        in_specs=(tokens, tokens) + (weights,) * 7 + (P(), rows, rows),
        out_specs=(tokens, tokens) + (weights,) * 7 + (P(),),
        check_vma=False,
    )
```

```python
import jax
import jax.numpy as jnp
from jax import lax
from jax.experimental import pallas as pl
from jax.experimental.pallas import tpu as pltpu
from jax.experimental.layout import Layout as Order, with_layout_constraint
from jax.sharding import Mesh, PartitionSpec as P

HEAD_DIM = 128
EPS = 1e-06
THETA = 500000.0
NEG = -1e30
F32 = jnp.float32
BF16 = jnp.bfloat16


def dot_rows_cols(left, right):
    return jnp.dot(left, right, preferred_element_type=F32)


def contract_cols(left, right):
    return lax.dot_general(left, right, (((1,), (1,)), ((), ())), preferred_element_type=F32)


def contract_rows(left, right):
    return lax.dot_general(left, right, (((0,), (0,)), ((), ())), preferred_element_type=F32)


def swap(values, axis):
    return lax.ppermute(values, axis, [(0, 1), (1, 0)])


def pick(flag, yes, no):
    return jnp.where(flag, yes, no)


def after(values, *done):
    return lax.optimization_barrier((values,) + done)[0] if done else values


class Net:
    def send(self, values, axis):
        return swap(values, axis)


def region(flag, step):
    out = jax.eval_shape(step)
    return lax.cond(flag, step, lambda: jax.tree.map(lambda leaf: jnp.zeros(leaf.shape, leaf.dtype), out))


def meet(*values):
    leaves, tree = jax.tree.flatten(values)
    return jax.tree.unflatten(tree, lax.optimization_barrier(tuple(leaves)))


class Sequence:
    def __init__(self):
        self.done = ()

    def wait(self, *received):
        self.done = self.done + received

    def run(self, step, *operands):
        if self.done:
            operands = lax.optimization_barrier(operands + self.done)[: len(operands)]
        out = step(*operands)
        self.done = out if isinstance(out, tuple) else (out,)
        return out


class Layout:
    def __init__(self, n_dp, n_tensor):
        self.dp_axes = tuple(f"d{i}" for i in range(n_dp.bit_length() - 1))
        self.tensor_axes = tuple(f"t{i}" for i in range(n_tensor.bit_length() - 1))
        self.col_axis = self.dp_axes[1]
        self.far = self.dp_axes[0]
        self.near = tuple(a for a in self.dp_axes if a not in (self.far, self.col_axis))
        self.core, self.side = self.tensor_axes[1], self.tensor_axes[0]
        self.n_dp = n_dp
        self.n_bits = len(self.dp_axes)

    def shape_of(self):
        return (2,) * (len(self.dp_axes) + len(self.tensor_axes))

    def dp_mask(self, axis):
        return 1 << (self.n_bits - 1 - self.dp_axes.index(axis))

    def block_order(self):
        order = []
        for j in range(1 << len(self.near)):
            block = sum(self.dp_mask(axis) for i, axis in enumerate(self.near) if (j >> i) & 1)
            for ahead in (0, self.dp_mask(self.far)):
                order += [block | ahead, block | ahead | self.dp_mask(self.col_axis)]
        return order

    def flip_blocks(self, blocks):
        for axis in self.near:
            flag, mask = lax.axis_index(axis) == 1, self.dp_mask(axis)
            blocks = [pick(flag, blocks[b ^ mask], blocks[b]) for b in range(len(blocks))]
        return blocks

    def to_relative(self, values):
        width = values.shape[-1] // self.n_dp
        blocks = [values[..., b * width : (b + 1) * width] for b in range(self.n_dp)]
        blocks = self.flip_blocks(blocks)
        return jnp.concatenate([blocks[b] for b in self.block_order()], -1)

    def from_relative(self, values):
        width = values.shape[-1] // self.n_dp
        blocks = [None] * self.n_dp
        for place, b in enumerate(self.block_order()):
            blocks[b] = values[..., place * width : (place + 1) * width]
        return jnp.concatenate(self.flip_blocks(blocks), -1)


def rope_tables(pos_col):
    lane = jnp.arange(HEAD_DIM, dtype=jnp.int32)[None, :]
    pair = (lane % (HEAD_DIM // 2)).astype(F32)
    inverse = THETA ** (-(pair * 2.0 / HEAD_DIM))
    angles = pos_col.astype(F32) * inverse
    return jnp.cos(angles), jnp.sin(angles) * jnp.where(lane < HEAD_DIM // 2, -1.0, 1.0)


def load_rows(ref):
    values = ref[...]
    return values.reshape(-1, values.shape[-1])


def head_scores(q_ref, k_ref, norm_ref, gain_q_ref, gain_k_ref, cos_ref, sin_ref, mask_ref):
    norms, cos_tab, sin_tab = load_rows(norm_ref), load_rows(cos_ref), load_rows(sin_ref)

    def rotated(values, gain):
        values = values * gain
        return (values * cos_tab + pltpu.roll(values, HEAD_DIM // 2, 1) * sin_tab).astype(BF16)

    query_hat = load_rows(q_ref) * norms[:, 0:1]
    key_hat = load_rows(k_ref) * norms[:, 1:2]
    q_rot = rotated(query_hat, gain_q_ref[...])
    k_rot = rotated(key_hat, gain_k_ref[...])
    scores = contract_cols(q_rot, k_rot) * HEAD_DIM ** (-0.5)
    scores = jnp.where(mask_ref[0] > 0, scores, NEG)
    exp_scores = jnp.exp(scores - jnp.max(scores, -1, keepdims=True))
    probs = exp_scores / jnp.sum(exp_scores, -1, keepdims=True)
    return query_hat, key_hat, q_rot, k_rot, probs, cos_tab, sin_tab


def attend_kernel(q_ref, k_ref, v_ref, norm_ref, gain_q_ref, gain_k_ref, cos_ref, sin_ref, mask_ref, out_ref):
    probs = head_scores(q_ref, k_ref, norm_ref, gain_q_ref, gain_k_ref, cos_ref, sin_ref, mask_ref)[4]
    out = dot_rows_cols(probs.astype(BF16), load_rows(v_ref).astype(BF16)).astype(BF16)
    out_ref[...] = out.reshape(out_ref.shape)


def attend_back_kernel(
    q_ref, k_ref, v_ref, norm_ref, gain_q_ref, gain_k_ref, cos_ref, sin_ref, mask_ref, grad_ref,
    grad_q_ref, grad_k_ref, grad_v_ref, inner_ref, gains_ref,
):
    query_hat, key_hat, q_rot, k_rot, probs, cos_tab, sin_tab = head_scores(
        q_ref, k_ref, norm_ref, gain_q_ref, gain_k_ref, cos_ref, sin_ref, mask_ref
    )
    grad_head = load_rows(grad_ref)
    grad_prob = contract_cols(grad_head, load_rows(v_ref).astype(BF16))
    row_dot = jnp.sum(probs * grad_prob, -1, keepdims=True)
    grad_scores = (probs * (grad_prob - row_dot)).astype(BF16)
    scale = HEAD_DIM ** (-0.5)

    def unrotated(values):
        return values * cos_tab - pltpu.roll(values, HEAD_DIM // 2, 1) * sin_tab

    grad_q = unrotated(dot_rows_cols(grad_scores, k_rot) * scale)
    grad_k = unrotated(contract_rows(grad_scores, q_rot) * scale)
    grad_v = contract_rows(probs.astype(BF16), grad_head).astype(BF16)
    product_q, product_k = grad_q * query_hat, grad_k * key_hat
    inner_q = jnp.sum(product_q * gain_q_ref[...], -1, keepdims=True)
    inner_k = jnp.sum(product_k * gain_k_ref[...], -1, keepdims=True)
    grad_q_ref[...] = grad_q.reshape(grad_q_ref.shape)
    grad_k_ref[...] = grad_k.reshape(grad_k_ref.shape)
    grad_v_ref[...] = grad_v.reshape(grad_v_ref.shape)
    inner_ref[...] = jnp.concatenate([inner_q, inner_k], 1).reshape(inner_ref.shape)
    gains_ref[...] = jnp.concatenate(
        [jnp.sum(product_q, 0, keepdims=True), jnp.sum(product_k, 0, keepdims=True)], 0
    ).reshape(gains_ref.shape)


def attention(qkv, norms, gain_query, gain_key, cos_tab, sin_tab, mask, grad_heads=None):
    n_tokens = qkv.shape[0]
    rows, n_heads = n_tokens // 4, qkv.shape[1] // (3 * HEAD_DIM)

    def split(values):
        return values.reshape(2, 2, rows, values.shape[-1])

    def columns(first):
        return pl.BlockSpec((2, 1, rows, HEAD_DIM), lambda s, h: (0, s, 0, first + h))

    def whole(width):
        return pl.BlockSpec((2, 1, rows, width), lambda s, h: (0, s, 0, 0))

    gain = pl.BlockSpec((1, HEAD_DIM), lambda s, h: (0, h))
    in_specs = [columns(0), columns(n_heads), columns(2 * n_heads), whole(2), gain, gain, whole(HEAD_DIM), whole(HEAD_DIM)]
    in_specs.append(pl.BlockSpec((1, 2 * rows, 2 * rows), lambda s, h: (s, 0, 0)))
    heads = split(qkv)
    operands = [heads, heads, heads, split(norms), gain_query[None], gain_key[None], split(cos_tab), split(sin_tab), mask]
    shape = (2, 2, rows, n_heads * HEAD_DIM)
    kernel, out_specs, out_shape = attend_kernel, columns(0), jax.ShapeDtypeStruct(shape, BF16)
    if grad_heads is not None:
        in_specs.append(columns(0))
        operands.append(split(grad_heads))
        kernel = attend_back_kernel
        out_specs = (
            columns(0),
            columns(0),
            columns(0),
            pl.BlockSpec((1, 2, 1, rows, 2), lambda s, h: (h, 0, s, 0, 0)),
            pl.BlockSpec((1, 2, HEAD_DIM), lambda s, h: (s, 0, h)),
        )
        out_shape = (
            jax.ShapeDtypeStruct(shape, F32),
            jax.ShapeDtypeStruct(shape, F32),
            jax.ShapeDtypeStruct(shape, BF16),
            jax.ShapeDtypeStruct((n_heads, 2, 2, rows, 2), F32),
            jax.ShapeDtypeStruct((2, 2, n_heads * HEAD_DIM), F32),
        )
    out = pl.pallas_call(
        kernel,
        grid=(2, n_heads),
        in_specs=in_specs,
        out_specs=out_specs,
        out_shape=out_shape,
        compiler_params=pltpu.CompilerParams(vmem_limit_bytes=48 * 1024 * 1024),
        cost_estimate=pl.CostEstimate(flops=1 << 30, bytes_accessed=1 << 23, transcendentals=1 << 20),
    )(*operands)
    if grad_heads is None:
        return out.reshape(n_tokens, -1)
    return tuple(part.reshape(n_tokens, -1) for part in out[:3]) + (out[3], jnp.sum(out[4], 0))


def block_program(lay):
    col, side, core = lay.col_axis, lay.side, lay.core

    def my(axis):
        return lax.axis_index(axis)

    def halves(weights):
        half = [w.shape[1] // 2 for w in weights]
        low = jnp.concatenate([w[:, :h] for w, h in zip(weights, half)], 1)
        high = jnp.concatenate([w[:, h:] for w, h in zip(weights, half)], 1)
        return low, high

    def leaving(weights):
        low, high = halves(weights)
        return pick(my(col) == 0, high, low)

    def both_rows(weights, got):
        low, high = halves(weights)
        first = my(col) == 0
        return jnp.concatenate([pick(first, low, got), pick(first, got, high)], 0)

    def ahead(block):
        return lax.all_gather(block, lay.far, axis=0, tiled=True)

    def beyond(both):
        half = both.shape[0] // 2
        return lax.dynamic_slice_in_dim(both, (1 - my(lay.far)) * half, half, 0)

    def in_two(own, other):
        first = my(lay.far) == 0
        return jnp.concatenate([pick(first, own, other), pick(first, other, own)], 0)

    def behind(total):
        return lax.psum_scatter(total.astype(BF16), lay.far, scatter_dimension=0, tiled=True)

    def spread(net, block):
        pieces = [block]
        for axis in lay.near:
            pieces = pieces + [net.send(piece, axis) for piece in pieces]
        return pieces

    def begin(net, grads):
        return [net.send(grad, lay.near[-1]) for grad in grads]

    def finish(net, keeps, received):
        pieces = [a.astype(F32) + b.astype(F32) for a, b in zip(keeps, received)]
        for axis in reversed(lay.near[:-1]):
            half = len(pieces) // 2
            others = [net.send(piece.astype(BF16), axis) for piece in pieces[half:]]
            pieces = [a + b.astype(F32) for a, b in zip(pieces[:half], others)]
        return pieces[0].astype(BF16)

    def to_leave(total):
        half = total.shape[0] // 2
        return pick(my(col) == 0, total[half:], total[:half]).astype(BF16)

    def owned(total, got):
        half = total.shape[0] // 2
        first = my(col) == 0
        mine, got = pick(first, total[:half], total[half:]), got.astype(F32)
        return pick(first, mine, got), pick(first, got, mine)

    def gather_begin(net, own):
        half = own.shape[0] // 2
        a0, b0 = own[:half], own[half:]
        return a0, b0, net.send(a0, side), net.send(b0, col)

    def gather_middle(net, state):
        a0, b0, a_side, b_col = state
        half = a0.shape[0]
        a_far = net.send(jnp.concatenate([a0, a_side], 0), col)
        b_far = net.send(jnp.concatenate([b0, b_col], 0), side)
        return [a0, b0, a_side, b_far[:half], a_far[:half], b_col, a_far[half:], b_far[half:]], (a_far, b_far)

    def gather_end(net, state):
        mine = jnp.concatenate(state[0], 0)
        other = net.send(mine, core)
        return jnp.concatenate([mine, other], 0), other

    def scatter_begin(net, product, n_rows):
        half = n_rows // 2
        received = net.send(product(slice(half, None)).astype(BF16), core)
        return product(slice(half)), received

    def scatter_second(net, state):
        part = state[0] + state[1].astype(F32)
        half = part.shape[0] // 8
        a0, b0, a_side, b_side, a_col, b_col, a_both, b_both = (part[i * half : (i + 1) * half] for i in range(8))
        received = (
            net.send(jnp.concatenate([a_col, a_both], 0).astype(BF16), col),
            net.send(jnp.concatenate([b_side, b_both], 0).astype(BF16), side),
        )
        return jnp.concatenate([a0, a_side], 0), jnp.concatenate([b0, b_col], 0), received

    def scatter_third(net, state):
        a_sum, b_sum = (own + got.astype(F32) for own, got in zip(state[:2], state[2]))
        half = a_sum.shape[0] // 2
        received = net.send(a_sum[half:].astype(BF16), side), net.send(b_sum[half:].astype(BF16), col)
        return a_sum[:half], b_sum[:half], received

    def scatter_end(state):
        a0, b0, received = state
        return jnp.concatenate([a0 + received[0].astype(F32), b0 + received[1].astype(F32)], 0)

    def token_rows(values, exchange):
        quarters = values.reshape(4, -1)
        rows = [quarters[0:1], quarters[1:2], quarters[2:3], quarters[3:4]]
        for axis, mask in ((side, 2), (core, 1)):
            flag = my(axis) == 1
            rows = [pick(flag, rows[i ^ mask], rows[i]) for i in range(4)]
        own = jnp.concatenate(rows, 0)
        other = exchange(own)
        order = [own[0:1], own[2:3], other[0:1], other[2:3], own[1:2], own[3:4], other[1:2], other[3:4]]
        return jnp.concatenate(order, 0)

    def token_rows_of(positions, seg_ids, net):
        rows = []

        def exchange(own):
            rows.append(own)
            return own

        token_rows(positions, exchange)
        token_rows(seg_ids, exchange)
        other = net.send(jnp.concatenate(rows, 0), col)
        return [
            token_rows(values, lambda own, i=i: other[4 * i : 4 * i + 4])
            for i, values in enumerate((positions, seg_ids))
        ]

    def add_all(net, values, axes):
        for axis in axes:
            received = net.send(values, axis)
            values = values + received
        return values

    def add_stats(net, rows):
        rows = rows.reshape(-1, 2, 2, 2, rows.shape[1] // 8)
        for dim, axis in ((1, core), (2, col), (3, side)):
            received = net.send(rows, axis)
            rows = rows + jnp.flip(received, dim)
        return rows.reshape(rows.shape[0], -1), received

    def on_device(
        hidden_in, out_grad, w_query, w_key, w_value, w_out, w_gate, w_up, w_down, gains, seg_ids, positions
    ):
        model_width = hidden_in.shape[1]
        head_cols = w_query.shape[1] // 2
        n_heads = head_cols // HEAD_DIM
        n_tokens = hidden_in.shape[0] * 8
        seq_len = n_tokens // 2
        score_scale = HEAD_DIM ** (-0.5)
        place = my(side) * 4 + my(core) * 2 + my(col)
        offset = place * head_cols
        per = seq_len // 4

        def by_seq(rows):
            return rows.reshape(2, 2, 2 * per).transpose(1, 0, 2).reshape(2, seq_len)

        net = Net()
        flag = positions[0] >= 0
        n_near = 1 << len(lay.near)
        piece = model_width // n_near
        kept_pieces, sent_pieces = range(n_near // 2), range(n_near // 2, n_near)

        def stack(*parts):
            return jnp.concatenate(parts, 0)

        def by_rows(left, pieces, cols=slice(None)):
            return sum(
                dot_rows_cols(left[:, j * piece : (j + 1) * piece], block[:, cols]) for j, block in enumerate(pieces)
            )

        def weight_grad(seq, left, right, which, cols=slice(None)):
            return [
                seq.run(
                    lambda a, b, j=j: contract_rows(a[:, j * piece : (j + 1) * piece], b[:, cols]).astype(BF16),
                    left,
                    right,
                )
                for j in which
            ]

        attn_weights = [w_query, w_key, w_value, w_out]

        def part_first():
            block_attn = both_rows(attn_weights, net.send(leaving(attn_weights), col))
            return block_attn, leaving([w_gate]), leaving([w_up]), lay.to_relative(hidden_in)

        block_attn, leave_gate, leave_up, x_low = region(flag, part_first)
        far_attn, own_attn = ahead(block_attn), spread(net, block_attn)[1:]

        def part_tokens():
            state = gather_begin(net, x_low)
            got_gate = net.send(after(leave_gate, *state[2:]), col)
            state = gather_middle(net, (*state[:3], after(state[3], got_gate)))
            tables = token_rows_of(positions, seg_ids, net)
            return state, leaving([w_down]), both_rows([w_gate], got_gate), tables

        out = region(flag, part_tokens)
        far_attn, own_attn, (state, leave_down, block_gate, (pos_rows, seg_rows)) = meet(far_attn, own_attn, out)
        got_up = net.send(leave_up, col)
        relay_attn = spread(net, beyond(far_attn))[1:]
        far_gate = ahead(block_gate)

        def part_tables():
            x_all, _ = gather_end(net, state)
            cos_tab, sin_tab = rope_tables(pos_rows.reshape(n_tokens, 1))
            ids_rows = token_rows(jnp.arange(seq_len, dtype=jnp.int32), lambda rows: rows)
            seg_seq, ids_seq = by_seq(seg_rows), by_seq(ids_rows)
            mask = (seg_seq[:, :, None] == seg_seq[:, None, :]) & (ids_seq[:, :, None] >= ids_seq[:, None, :])
            mask = mask.astype(F32)
            gain_query = lax.dynamic_slice_in_dim(gains[0], offset, head_cols)
            gain_key = lax.dynamic_slice_in_dim(gains[1], offset, head_cols)
            gain_post = lay.to_relative(gains[2:4])
            more = gain_query, gain_key, gain_post[0:1], gain_post[1:2], lay.to_relative(out_grad).astype(F32)
            return x_all, cos_tab, sin_tab, mask, more

        out = region(flag, part_tables)
        relay_attn, got_up, (x_all, cos_tab, sin_tab, mask, more) = meet(relay_attn, got_up, out)
        gain_query, gain_key, gain_attn, gain_mlp, grad_out = more
        block_up = both_rows([w_up], got_up)
        far_up, own_up = ahead(block_up), spread(net, block_up)[1:]
        qkv_cols, out_cols = slice(3 * head_cols), slice(3 * head_cols, None)


        def part_qkv():
            near_attn = [far_attn, *(in_two(own, other) for own, other in zip(own_attn, relay_attn))]
            qkv = with_layout_constraint(by_rows(x_all, near_attn, qkv_cols), Order((0, 1)))
            squares, _ = add_stats(
                net,
                jnp.stack(
                    [jnp.sum(part * part, -1) for part in (qkv[:, :head_cols], qkv[:, head_cols : 2 * head_cols])], 0
                ),
            )
            return near_attn, qkv, squares, stack(*(block[:, out_cols] for block in near_attn))

        out = region(flag, part_qkv)
        leave_down, (near_attn, qkv, squares, out_w) = meet(leave_down, out)
        got_down = net.send(leave_down, col)

        def part_attend():
            norms = lax.rsqrt(squares / model_width + EPS).T
            attn_low = attention(qkv, norms, gain_query, gain_key, cos_tab, sin_tab, mask)
            state = scatter_begin(net, lambda rows: contract_cols(attn_low[rows], out_w), n_tokens)
            return attn_low, norms, state

        out = region(flag, part_attend)
        own_up, far_gate, got_down, (attn_low, norms, state) = meet(own_up, far_gate, got_down, out)
        near_gate = spread(net, far_gate)
        block_down = both_rows([w_down], got_down)
        far_down = ahead(block_down)

        def part_resid():
            attn_sum = scatter_end(scatter_third(net, scatter_second(net, state)))
            norm_attn = lax.rsqrt(jnp.mean(attn_sum * attn_sum, -1, keepdims=True) + EPS)
            attn_hat = attn_sum * norm_attn
            resid = x_low.astype(F32) + attn_hat * gain_attn
            return norm_attn, attn_hat, resid, gather_begin(net, resid.astype(BF16))

        out = region(flag, part_resid)
        near_gate, far_up, (norm_attn, attn_hat, resid, state) = meet(near_gate, far_up, out)
        relay_up = spread(net, beyond(far_up))[1:]
        own_down = spread(net, block_down)[1:]

        def part_gate():
            mlp_in, _ = gather_end(net, gather_middle(net, state))
            return mlp_in, by_rows(mlp_in, near_gate)

        out = region(flag, part_gate)
        relay_up, own_down, far_down, (mlp_in, gate_proj) = meet(relay_up, own_down, far_down, out)
        relay_down = spread(net, beyond(far_down))[1:]

        def part_up():
            near_up = [far_up, *(in_two(own, other) for own, other in zip(own_up, relay_up))]
            up_proj = by_rows(mlp_in, near_up)
            hidden_act = (gate_proj * jax.nn.sigmoid(gate_proj) * up_proj).astype(BF16)
            return up_proj, hidden_act, near_up

        out = region(flag, part_up)
        relay_down, (up_proj, hidden_act, near_up) = meet(relay_down, out)

        act_halves = slice(hidden_act.shape[1] // 2), slice(hidden_act.shape[1] // 2, None)

        def part_down():
            down_w = stack(far_down, *(in_two(own, other) for own, other in zip(own_down, relay_down)))
            state = scatter_begin(net, lambda rows: contract_cols(hidden_act[rows], down_w), n_tokens)
            mlp_sum = scatter_end(scatter_third(net, scatter_second(net, state)))
            norm_mlp = lax.rsqrt(jnp.mean(mlp_sum * mlp_sum, -1, keepdims=True) + EPS)
            mlp_hat = mlp_sum * norm_mlp
            scaled = grad_out * gain_mlp
            grad_mlp = norm_mlp * (scaled - mlp_hat * jnp.mean(mlp_hat * scaled, -1, keepdims=True))
            grad_mlp_all, _ = gather_end(net, gather_middle(net, gather_begin(net, grad_mlp.astype(BF16))))
            seq = Sequence()
            sends = weight_grad(seq, grad_mlp_all, hidden_act, sent_pieces, act_halves[0])
            return down_w, mlp_hat, grad_mlp_all, sends, stack(*near_gate), stack(*near_up)

        down_w, mlp_hat, grad_mlp_all, sends, gate_w, up_w = region(flag, part_down)
        got_first = begin(net, sends)

        def part_back_act():
            seq = Sequence()
            keeps_first = weight_grad(seq, grad_mlp_all, hidden_act, kept_pieces, act_halves[0])

            def back_act(grad_mlp_all, down_w):
                sig_gate = jax.nn.sigmoid(gate_proj)
                grad_act = dot_rows_cols(grad_mlp_all, down_w)
                grad_gate = (grad_act * up_proj * (sig_gate * (1.0 + gate_proj * (1.0 - sig_gate)))).astype(BF16)
                return grad_gate, (grad_act * (gate_proj * sig_gate)).astype(BF16)

            grad_gate, grad_up = seq.run(back_act, grad_mlp_all, down_w)
            down_sends = weight_grad(seq, grad_mlp_all, hidden_act, sent_pieces, act_halves[1])
            gate_sends = weight_grad(seq, mlp_in, grad_gate, sent_pieces)
            return keeps_first, grad_gate, grad_up, down_sends, gate_sends

        out = region(flag, part_back_act)
        got_first, (keeps_first, grad_gate, grad_up, down_sends, gate_sends) = meet(got_first, out)
        got_second, got_gate = begin(net, down_sends), begin(net, gate_sends)
        down_first = behind(finish(net, keeps_first, got_first))

        def part_back_resid():
            seq = Sequence()
            state = scatter_begin(
                net,
                lambda rows: seq.run(
                    lambda a, b, c, d: contract_cols(a[rows], c) + contract_cols(b[rows], d),
                    grad_gate,
                    grad_up,
                    gate_w,
                    up_w,
                ),
                n_tokens,
            )
            return weight_grad(seq, grad_mlp_all, hidden_act, kept_pieces, act_halves[1]), state

        out = region(flag, part_back_resid)
        got_second, (keeps_second, state) = meet(got_second, out)
        down_second = behind(finish(net, keeps_second, got_second))

        def part_back_attn():
            seq = Sequence()
            later = scatter_second(net, state)
            keeps_gate = weight_grad(seq, mlp_in, grad_gate, kept_pieces)
            seq.wait(*later[2])
            later = scatter_third(net, later)
            sends = weight_grad(seq, mlp_in, grad_up, sent_pieces)
            seq.wait(*later[2])
            grad_resid = grad_out + scatter_end(later)
            scaled = grad_resid * gain_attn
            grad_attn = norm_attn * (scaled - attn_hat * jnp.mean(attn_hat * scaled, -1, keepdims=True))
            first = gather_begin(net, grad_attn.astype(BF16))
            gain_row_attn = jnp.sum(grad_resid * attn_hat, 0, keepdims=True)
            keeps_up = weight_grad(seq, mlp_in, grad_up, kept_pieces)
            return keeps_gate, sends, keeps_up, grad_resid, first, gain_row_attn

        out = region(flag, part_back_attn)
        got_gate, down_first, out = meet(got_gate, down_first, out)
        keeps_gate, sends, keeps_up, grad_resid, state, gain_row_attn = out
        got_up = begin(net, sends)
        total_gate = behind(finish(net, keeps_gate, got_gate))

        def part_back_heads():
            grad_attn_all, _ = gather_end(net, gather_middle(net, state))
            grad_heads = dot_rows_cols(grad_attn_all, out_w).astype(BF16)
            return grad_attn_all, attention(qkv, norms, gain_query, gain_key, cos_tab, sin_tab, mask, grad_heads)

        out = region(flag, part_back_heads)
        got_up, down_second, (grad_attn_all, grads) = meet(got_up, down_second, out)
        grad_query_n, grad_key_n, grad_value_low, inner_parts, head_gains = grads
        total_up = behind(finish(net, keeps_up, got_up))

        def part_back_value():
            seq = Sequence()
            inner, received = add_stats(net, jnp.sum(inner_parts, 0).reshape(n_tokens, 2).T)
            sends = [
                jnp.concatenate(pair, 1)
                for pair in zip(
                    weight_grad(seq, x_all, grad_value_low, sent_pieces),
                    weight_grad(seq, grad_attn_all, attn_low, sent_pieces),
                )
            ]
            total_down = jnp.concatenate([down_first, down_second], 1)
            return inner, sends, total_down, to_leave(total_down)

        inner, sends, total_down, leave = region(flag, part_back_value)
        got_first, got_down = begin(net, sends), net.send(leave, col)

        def part_back_qkv():
            seq = Sequence()
            qkv_w = stack(*(part[:, qkv_cols] for part in near_attn))
            keeps_first = [
                jnp.concatenate(pair, 1)
                for pair in zip(
                    weight_grad(seq, x_all, grad_value_low, kept_pieces),
                    weight_grad(seq, grad_attn_all, attn_low, kept_pieces),
                )
            ]
            scale = inner.T / model_width

            def through_norm(grad, i, gain):
                hat = qkv[:, i * head_cols : (i + 1) * head_cols] * norms[:, i : i + 1]
                return (norms[:, i : i + 1] * (grad * gain - hat * scale[:, i : i + 1])).astype(BF16)

            qk_right = seq.run(
                lambda a, b: jnp.concatenate(
                    [through_norm(a, 0, gain_query), through_norm(b, 1, gain_key)], 1
                ),
                grad_query_n,
                grad_key_n,
            )
            return qk_right, keeps_first, weight_grad(seq, x_all, qk_right, sent_pieces), qkv_w

        out = region(flag, part_back_qkv)
        got_first, total_gate, (qk_right, keeps_first, sends, qkv_w) = meet(got_first, total_gate, out)
        got_second = begin(net, sends)
        vo_total = behind(finish(net, keeps_first, got_first))
        got_gate = net.send(to_leave(total_gate), col)

        def part_in_part():
            keeps_second = weight_grad(Sequence(), x_all, qk_right, kept_pieces)
            qkv_right = jnp.concatenate([qk_right, grad_value_low], 1)
            head_rows = lax.dynamic_update_slice(
                jnp.zeros((2, model_width), F32), head_gains, (jnp.int32(0), offset)
            )
            gain_row_mlp = jnp.sum(grad_out * mlp_hat, 0, keepdims=True)
            post_rows = lay.from_relative(jnp.concatenate([gain_row_attn, gain_row_mlp], 0))
            gain_rows = add_all(net, jnp.concatenate([head_rows, post_rows], 0), (side, core))
            return keeps_second, scatter_begin(net, lambda rows: contract_cols(qkv_right[rows], qkv_w), n_tokens), gain_rows

        out = region(flag, part_in_part)
        got_second, got_down, got_gate, total_up, out = meet(got_second, got_down, got_gate, total_up, out)
        keeps_second, state, gain_rows = out
        got_up = net.send(to_leave(total_up), col)
        qk_total = behind(finish(net, keeps_second, got_second))

        def part_outputs():
            ending = scatter_third(net, scatter_second(net, state))
            gate_grad = jnp.concatenate(owned(total_gate, got_gate), 1)
            down_grad = jnp.concatenate(owned(total_down, got_down), 1)
            hidden_out = lay.from_relative((resid + mlp_hat * gain_mlp).astype(BF16))
            near_rows = add_all(net, gain_rows, lay.near)
            return ending, gate_grad, down_grad, hidden_out, near_rows

        out = region(flag, part_outputs)
        vo_total, qk_total, got_up, out = meet(vo_total, qk_total, got_up, out)
        state, gate_grad, down_grad, hidden_out, gain_rows = out
        got_vo, got_qk = net.send(to_leave(vo_total), col), net.send(to_leave(qk_total), col)

        def part_last():
            gains_grad = add_all(net, gain_rows, (lay.far, lay.col_axis))
            up_grad = jnp.concatenate(owned(total_up, got_up), 1)
            return lay.from_relative(grad_resid + scatter_end(state)), up_grad, gains_grad

        out = region(flag, part_last)
        got_vo, got_qk, (in_grad, up_grad, gains_grad) = meet(got_vo, got_qk, out)
        vo_pair = owned(vo_total, got_vo)
        qk_pair = owned(qk_total, got_qk)
        query_grad, key_grad, value_grad, out_grad_own = (
            jnp.concatenate([part[:, i * head_cols : (i + 1) * head_cols] for part in pair], 1)
            for pair in (qk_pair, vo_pair)
            for i in range(2)
        )
        return (
            hidden_out,
            in_grad,
            query_grad,
            key_grad,
            value_grad,
            out_grad_own,
            gate_grad,
            up_grad,
            down_grad,
            gains_grad,
        )

    return on_device


def solution(mesh):
    lay = Layout(mesh.shape["dp"], mesh.shape["tensor"])
    fine = Mesh(mesh.devices.reshape(lay.shape_of()), lay.dp_axes + lay.tensor_axes)
    tokens = P(lay.dp_axes + lay.tensor_axes, None)
    weights = P(lay.dp_axes, lay.tensor_axes)
    rows = P(lay.dp_axes)
    return jax.shard_map(
        block_program(lay),
        mesh=fine,
        in_specs=(tokens, tokens) + (weights,) * 7 + (P(), rows, rows),
        out_specs=(tokens, tokens) + (weights,) * 7 + (P(),),
        check_vma=False,
    )
```

```python
import jax
import jax.numpy as jnp
from jax import lax
from jax.experimental import pallas as pl
from jax.experimental.pallas import tpu as pltpu
from jax.experimental.layout import Layout as Order, with_layout_constraint
from jax.sharding import Mesh, PartitionSpec as P

HEAD_DIM = 128
EPS = 1e-06
THETA = 500000.0
NEG = -1e30
F32 = jnp.float32
BF16 = jnp.bfloat16


def dot_rows_cols(left, right):
    return jnp.dot(left, right, preferred_element_type=F32)


def contract_cols(left, right):
    return lax.dot_general(left, right, (((1,), (1,)), ((), ())), preferred_element_type=F32)


def contract_rows(left, right):
    return lax.dot_general(left, right, (((0,), (0,)), ((), ())), preferred_element_type=F32)


def swap(values, axis):
    return lax.ppermute(values, axis, [(0, 1), (1, 0)])


def pick(flag, yes, no):
    return jnp.where(flag, yes, no)


def after(values, *done):
    return lax.optimization_barrier((values,) + done)[0] if done else values


class Net:
    def send(self, values, axis):
        return swap(values, axis)


def region(flag, step):
    out = jax.eval_shape(step)
    return lax.cond(flag, step, lambda: jax.tree.map(lambda leaf: jnp.zeros(leaf.shape, leaf.dtype), out))


def meet(*values):
    leaves, tree = jax.tree.flatten(values)
    return jax.tree.unflatten(tree, lax.optimization_barrier(tuple(leaves)))


class Sequence:
    def __init__(self):
        self.done = ()

    def wait(self, *received):
        self.done = self.done + received

    def run(self, step, *operands):
        if self.done:
            operands = lax.optimization_barrier(operands + self.done)[: len(operands)]
        out = step(*operands)
        self.done = out if isinstance(out, tuple) else (out,)
        return out


class Layout:
    def __init__(self, n_dp, n_tensor):
        self.dp_axes = tuple(f"d{i}" for i in range(n_dp.bit_length() - 1))
        self.tensor_axes = tuple(f"t{i}" for i in range(n_tensor.bit_length() - 1))
        self.col_axis = self.dp_axes[1]
        self.far = self.dp_axes[0]
        self.near = tuple(a for a in self.dp_axes if a not in (self.far, self.col_axis))
        self.core, self.side = self.tensor_axes[1], self.tensor_axes[0]
        self.n_dp = n_dp
        self.n_bits = len(self.dp_axes)

    def shape_of(self):
        return (2,) * (len(self.dp_axes) + len(self.tensor_axes))

    def dp_mask(self, axis):
        return 1 << (self.n_bits - 1 - self.dp_axes.index(axis))

    def block_order(self):
        order = []
        for j in range(1 << len(self.near)):
            block = sum(self.dp_mask(axis) for i, axis in enumerate(self.near) if (j >> i) & 1)
            for ahead in (0, self.dp_mask(self.far)):
                order += [block | ahead, block | ahead | self.dp_mask(self.col_axis)]
        return order

    def flip_blocks(self, blocks):
        for axis in self.near:
            flag, mask = lax.axis_index(axis) == 1, self.dp_mask(axis)
            blocks = [pick(flag, blocks[b ^ mask], blocks[b]) for b in range(len(blocks))]
        return blocks

    def to_relative(self, values):
        width = values.shape[-1] // self.n_dp
        blocks = [values[..., b * width : (b + 1) * width] for b in range(self.n_dp)]
        blocks = self.flip_blocks(blocks)
        return jnp.concatenate([blocks[b] for b in self.block_order()], -1)

    def from_relative(self, values):
        width = values.shape[-1] // self.n_dp
        blocks = [None] * self.n_dp
        for place, b in enumerate(self.block_order()):
            blocks[b] = values[..., place * width : (place + 1) * width]
        return jnp.concatenate(self.flip_blocks(blocks), -1)


def rope_tables(pos_col):
    lane = jnp.arange(HEAD_DIM, dtype=jnp.int32)[None, :]
    pair = (lane % (HEAD_DIM // 2)).astype(F32)
    inverse = THETA ** (-(pair * 2.0 / HEAD_DIM))
    angles = pos_col.astype(F32) * inverse
    return jnp.cos(angles), jnp.sin(angles) * jnp.where(lane < HEAD_DIM // 2, -1.0, 1.0)


def load_rows(ref):
    values = ref[...]
    return values.reshape(-1, values.shape[-1])


def head_scores(q_ref, k_ref, norm_ref, gain_q_ref, gain_k_ref, cos_ref, sin_ref, mask_ref):
    norms, cos_tab, sin_tab = load_rows(norm_ref), load_rows(cos_ref), load_rows(sin_ref)

    def rotated(values, gain):
        values = values * gain
        return (values * cos_tab + pltpu.roll(values, HEAD_DIM // 2, 1) * sin_tab).astype(BF16)

    query_hat = load_rows(q_ref) * norms[:, 0:1]
    key_hat = load_rows(k_ref) * norms[:, 1:2]
    q_rot = rotated(query_hat, gain_q_ref[...])
    k_rot = rotated(key_hat, gain_k_ref[...])
    scores = contract_cols(q_rot, k_rot) * HEAD_DIM ** (-0.5)
    scores = jnp.where(mask_ref[0] > 0, scores, NEG)
    exp_scores = jnp.exp(scores - jnp.max(scores, -1, keepdims=True))
    probs = exp_scores / jnp.sum(exp_scores, -1, keepdims=True)
    return query_hat, key_hat, q_rot, k_rot, probs, cos_tab, sin_tab


def attend_kernel(q_ref, k_ref, v_ref, norm_ref, gain_q_ref, gain_k_ref, cos_ref, sin_ref, mask_ref, out_ref):
    probs = head_scores(q_ref, k_ref, norm_ref, gain_q_ref, gain_k_ref, cos_ref, sin_ref, mask_ref)[4]
    out = dot_rows_cols(probs.astype(BF16), load_rows(v_ref).astype(BF16)).astype(BF16)
    out_ref[...] = out.reshape(out_ref.shape)


def attend_back_kernel(
    q_ref, k_ref, v_ref, norm_ref, gain_q_ref, gain_k_ref, cos_ref, sin_ref, mask_ref, grad_ref,
    grad_q_ref, grad_k_ref, grad_v_ref, inner_ref, gains_ref,
):
    query_hat, key_hat, q_rot, k_rot, probs, cos_tab, sin_tab = head_scores(
        q_ref, k_ref, norm_ref, gain_q_ref, gain_k_ref, cos_ref, sin_ref, mask_ref
    )
    grad_head = load_rows(grad_ref)
    grad_prob = contract_cols(grad_head, load_rows(v_ref).astype(BF16))
    row_dot = jnp.sum(probs * grad_prob, -1, keepdims=True)
    grad_scores = (probs * (grad_prob - row_dot)).astype(BF16)
    scale = HEAD_DIM ** (-0.5)

    def unrotated(values):
        return values * cos_tab - pltpu.roll(values, HEAD_DIM // 2, 1) * sin_tab

    grad_q = unrotated(dot_rows_cols(grad_scores, k_rot) * scale)
    grad_k = unrotated(contract_rows(grad_scores, q_rot) * scale)
    grad_v = contract_rows(probs.astype(BF16), grad_head).astype(BF16)
    product_q, product_k = grad_q * query_hat, grad_k * key_hat
    inner_q = jnp.sum(product_q * gain_q_ref[...], -1, keepdims=True)
    inner_k = jnp.sum(product_k * gain_k_ref[...], -1, keepdims=True)
    grad_q_ref[...] = grad_q.reshape(grad_q_ref.shape)
    grad_k_ref[...] = grad_k.reshape(grad_k_ref.shape)
    grad_v_ref[...] = grad_v.reshape(grad_v_ref.shape)
    inner_ref[...] = jnp.concatenate([inner_q, inner_k], 1).reshape(inner_ref.shape)
    gains_ref[...] = jnp.concatenate(
        [jnp.sum(product_q, 0, keepdims=True), jnp.sum(product_k, 0, keepdims=True)], 0
    ).reshape(gains_ref.shape)


def attention(qkv, norms, gain_query, gain_key, cos_tab, sin_tab, mask, grad_heads=None):
    n_tokens = qkv.shape[0]
    rows, n_heads = n_tokens // 4, qkv.shape[1] // (3 * HEAD_DIM)

    def split(values):
        return values.reshape(2, 2, rows, values.shape[-1])

    def columns(first):
        return pl.BlockSpec((2, 1, rows, HEAD_DIM), lambda s, h: (0, s, 0, first + h))

    def whole(width):
        return pl.BlockSpec((2, 1, rows, width), lambda s, h: (0, s, 0, 0))

    gain = pl.BlockSpec((1, HEAD_DIM), lambda s, h: (0, h))
    in_specs = [columns(0), columns(n_heads), columns(2 * n_heads), whole(2), gain, gain, whole(HEAD_DIM), whole(HEAD_DIM)]
    in_specs.append(pl.BlockSpec((1, 2 * rows, 2 * rows), lambda s, h: (s, 0, 0)))
    heads = split(qkv)
    operands = [heads, heads, heads, split(norms), gain_query[None], gain_key[None], split(cos_tab), split(sin_tab), mask]
    shape = (2, 2, rows, n_heads * HEAD_DIM)
    kernel, out_specs, out_shape = attend_kernel, columns(0), jax.ShapeDtypeStruct(shape, BF16)
    if grad_heads is not None:
        in_specs.append(columns(0))
        operands.append(split(grad_heads))
        kernel = attend_back_kernel
        out_specs = (
            columns(0),
            columns(0),
            columns(0),
            pl.BlockSpec((1, 2, 1, rows, 2), lambda s, h: (h, 0, s, 0, 0)),
            pl.BlockSpec((1, 2, HEAD_DIM), lambda s, h: (s, 0, h)),
        )
        out_shape = (
            jax.ShapeDtypeStruct(shape, F32),
            jax.ShapeDtypeStruct(shape, F32),
            jax.ShapeDtypeStruct(shape, BF16),
            jax.ShapeDtypeStruct((n_heads, 2, 2, rows, 2), F32),
            jax.ShapeDtypeStruct((2, 2, n_heads * HEAD_DIM), F32),
        )
    out = pl.pallas_call(
        kernel,
        grid=(2, n_heads),
        in_specs=in_specs,
        out_specs=out_specs,
        out_shape=out_shape,
        compiler_params=pltpu.CompilerParams(vmem_limit_bytes=48 * 1024 * 1024),
        cost_estimate=pl.CostEstimate(flops=1 << 30, bytes_accessed=1 << 23, transcendentals=1 << 20),
    )(*operands)
    if grad_heads is None:
        return out.reshape(n_tokens, -1)
    return tuple(part.reshape(n_tokens, -1) for part in out[:3]) + (out[3], jnp.sum(out[4], 0))


def block_program(lay):
    col, side, core = lay.col_axis, lay.side, lay.core

    def my(axis):
        return lax.axis_index(axis)

    def halves(weights):
        half = [w.shape[1] // 2 for w in weights]
        low = jnp.concatenate([w[:, :h] for w, h in zip(weights, half)], 1)
        high = jnp.concatenate([w[:, h:] for w, h in zip(weights, half)], 1)
        return low, high

    def leaving(weights):
        low, high = halves(weights)
        return pick(my(col) == 0, high, low)

    def both_rows(weights, got):
        low, high = halves(weights)
        first = my(col) == 0
        return jnp.concatenate([pick(first, low, got), pick(first, got, high)], 0)

    def ahead(block):
        return lax.all_gather(block, lay.far, axis=0, tiled=True)

    def beyond(both):
        half = both.shape[0] // 2
        return lax.dynamic_slice_in_dim(both, (1 - my(lay.far)) * half, half, 0)

    def in_two(own, other):
        first = my(lay.far) == 0
        return jnp.concatenate([pick(first, own, other), pick(first, other, own)], 0)

    def behind(total):
        return lax.psum_scatter(total.astype(BF16), lay.far, scatter_dimension=0, tiled=True)

    def spread(net, block):
        pieces = [block]
        for axis in lay.near:
            pieces = pieces + [net.send(piece, axis) for piece in pieces]
        return pieces

    def begin(net, grads):
        return [net.send(grad, lay.near[-1]) for grad in grads]

    def finish(net, keeps, received):
        pieces = [a.astype(F32) + b.astype(F32) for a, b in zip(keeps, received)]
        for axis in reversed(lay.near[:-1]):
            half = len(pieces) // 2
            others = [net.send(piece.astype(BF16), axis) for piece in pieces[half:]]
            pieces = [a + b.astype(F32) for a, b in zip(pieces[:half], others)]
        return pieces[0].astype(BF16)

    def to_leave(total):
        half = total.shape[0] // 2
        return pick(my(col) == 0, total[half:], total[:half]).astype(BF16)

    def owned(total, got):
        half = total.shape[0] // 2
        first = my(col) == 0
        mine, got = pick(first, total[:half], total[half:]), got.astype(F32)
        return pick(first, mine, got), pick(first, got, mine)

    def gather_begin(net, own):
        half = own.shape[0] // 2
        a0, b0 = own[:half], own[half:]
        return a0, b0, net.send(a0, side), net.send(b0, col)

    def gather_middle(net, state):
        a0, b0, a_side, b_col = state
        half = a0.shape[0]
        a_far = net.send(jnp.concatenate([a0, a_side], 0), col)
        b_far = net.send(jnp.concatenate([b0, b_col], 0), side)
        return [a0, b0, a_side, b_far[:half], a_far[:half], b_col, a_far[half:], b_far[half:]], (a_far, b_far)

    def gather_end(net, state):
        return gather_cores(net, jnp.concatenate(state[0], 0))

    def gather_cores(net, mine):
        other = net.send(mine, core)
        return jnp.concatenate([mine, other], 0), other

    def scatter_begin(net, product, n_rows):
        half = n_rows // 2
        received = net.send(product(slice(half, None)).astype(BF16), core)
        return product(slice(half)).astype(BF16), received

    def scatter_second(net, state):
        part = state[0].astype(F32) + state[1].astype(F32)
        half = part.shape[0] // 8
        a0, b0, a_side, b_side, a_col, b_col, a_both, b_both = (part[i * half : (i + 1) * half] for i in range(8))
        received = (
            net.send(jnp.concatenate([a_col, a_both], 0).astype(BF16), col),
            net.send(jnp.concatenate([b_side, b_both], 0).astype(BF16), side),
        )
        return jnp.concatenate([a0, a_side], 0), jnp.concatenate([b0, b_col], 0), received

    def scatter_third(net, state):
        a_sum, b_sum = (own + got.astype(F32) for own, got in zip(state[:2], state[2]))
        half = a_sum.shape[0] // 2
        received = net.send(a_sum[half:].astype(BF16), side), net.send(b_sum[half:].astype(BF16), col)
        return a_sum[:half], b_sum[:half], received

    def scatter_end(state):
        a0, b0, received = state
        return jnp.concatenate([a0 + received[0].astype(F32), b0 + received[1].astype(F32)], 0)

    def token_rows(values, exchange):
        quarters = values.reshape(4, -1)
        rows = [quarters[0:1], quarters[1:2], quarters[2:3], quarters[3:4]]
        for axis, mask in ((side, 2), (core, 1)):
            flag = my(axis) == 1
            rows = [pick(flag, rows[i ^ mask], rows[i]) for i in range(4)]
        own = jnp.concatenate(rows, 0)
        other = exchange(own)
        order = [own[0:1], own[2:3], other[0:1], other[2:3], own[1:2], own[3:4], other[1:2], other[3:4]]
        return jnp.concatenate(order, 0)

    def token_rows_of(positions, seg_ids, net):
        rows = []

        def exchange(own):
            rows.append(own)
            return own

        token_rows(positions, exchange)
        token_rows(seg_ids, exchange)
        other = net.send(jnp.concatenate(rows, 0), col)
        return [
            token_rows(values, lambda own, i=i: other[4 * i : 4 * i + 4])
            for i, values in enumerate((positions, seg_ids))
        ]

    def add_all(net, values, axes):
        for axis in axes:
            received = net.send(values, axis)
            values = values + received
        return values

    def add_stats(net, rows):
        rows = rows.reshape(-1, 2, 2, 2, rows.shape[1] // 8)
        for dim, axis in ((1, core), (2, col), (3, side)):
            received = net.send(rows, axis)
            rows = rows + jnp.flip(received, dim)
        return rows.reshape(rows.shape[0], -1), received

    def on_device(
        hidden_in, out_grad, w_query, w_key, w_value, w_out, w_gate, w_up, w_down, gains, seg_ids, positions
    ):
        model_width = hidden_in.shape[1]
        head_cols = w_query.shape[1] // 2
        n_heads = head_cols // HEAD_DIM
        n_tokens = hidden_in.shape[0] * 8
        seq_len = n_tokens // 2
        score_scale = HEAD_DIM ** (-0.5)
        place = my(side) * 4 + my(core) * 2 + my(col)
        offset = place * head_cols
        per = seq_len // 4

        def by_seq(rows):
            return rows.reshape(2, 2, 2 * per).transpose(1, 0, 2).reshape(2, seq_len)

        net = Net()
        flag = positions[0] >= 0
        n_near = 1 << len(lay.near)
        piece = model_width // n_near
        kept_pieces, sent_pieces = range(n_near // 2), range(n_near // 2, n_near)

        def stack(*parts):
            return jnp.concatenate(parts, 0)

        def by_rows(left, pieces, cols=slice(None)):
            return sum(
                dot_rows_cols(left[:, j * piece : (j + 1) * piece], block[:, cols]) for j, block in enumerate(pieces)
            )

        def weight_grad(seq, left, right, which, cols=slice(None)):
            return [
                seq.run(
                    lambda a, b, j=j: contract_rows(a[:, j * piece : (j + 1) * piece], b[:, cols]).astype(BF16),
                    left,
                    right,
                )
                for j in which
            ]

        attn_weights = [w_query, w_key, w_value, w_out]

        def part_first():
            block_attn = both_rows(attn_weights, net.send(leaving(attn_weights), col))
            return block_attn, leaving([w_gate]), leaving([w_up]), lay.to_relative(hidden_in)

        block_attn, leave_gate, leave_up, x_low = region(flag, part_first)
        far_attn, own_attn = ahead(block_attn), spread(net, block_attn)[1:]

        def part_tokens():
            state = gather_begin(net, x_low)
            got_gate = net.send(after(leave_gate, *state[2:]), col)
            state = gather_middle(net, (*state[:3], after(state[3], got_gate)))
            tables = token_rows_of(positions, seg_ids, net)
            return state, leaving([w_down]), both_rows([w_gate], got_gate), tables

        out = region(flag, part_tokens)
        far_attn, own_attn, (state, leave_down, block_gate, (pos_rows, seg_rows)) = meet(far_attn, own_attn, out)
        got_up = net.send(leave_up, col)
        relay_attn = spread(net, beyond(far_attn))[1:]
        far_gate = ahead(block_gate)

        def part_tables():
            x_all, _ = gather_end(net, state)
            cos_tab, sin_tab = rope_tables(pos_rows.reshape(n_tokens, 1))
            ids_rows = token_rows(jnp.arange(seq_len, dtype=jnp.int32), lambda rows: rows)
            seg_seq, ids_seq = by_seq(seg_rows), by_seq(ids_rows)
            mask = (seg_seq[:, :, None] == seg_seq[:, None, :]) & (ids_seq[:, :, None] >= ids_seq[:, None, :])
            mask = mask.astype(F32)
            gain_query = lax.dynamic_slice_in_dim(gains[0], offset, head_cols)
            gain_key = lax.dynamic_slice_in_dim(gains[1], offset, head_cols)
            gain_post = lay.to_relative(gains[2:4])
            more = gain_query, gain_key, gain_post[0:1], gain_post[1:2], lay.to_relative(out_grad).astype(F32)
            return x_all, cos_tab, sin_tab, mask, more

        out = region(flag, part_tables)
        relay_attn, got_up, (x_all, cos_tab, sin_tab, mask, more) = meet(relay_attn, got_up, out)
        gain_query, gain_key, gain_attn, gain_mlp, grad_out = more
        block_up = both_rows([w_up], got_up)
        far_up, own_up = ahead(block_up), spread(net, block_up)[1:]
        qkv_cols, out_cols = slice(3 * head_cols), slice(3 * head_cols, None)


        def part_qkv():
            near_attn = [far_attn, *(in_two(own, other) for own, other in zip(own_attn, relay_attn))]
            qkv = with_layout_constraint(by_rows(x_all, near_attn, qkv_cols), Order((0, 1)))
            squares, _ = add_stats(
                net,
                jnp.stack(
                    [jnp.sum(part * part, -1) for part in (qkv[:, :head_cols], qkv[:, head_cols : 2 * head_cols])], 0
                ),
            )
            return near_attn, qkv, squares, stack(*(block[:, out_cols] for block in near_attn))

        out = region(flag, part_qkv)
        leave_down, (near_attn, qkv, squares, out_w) = meet(leave_down, out)
        got_down = net.send(leave_down, col)

        def part_attend():
            norms = lax.rsqrt(squares / model_width + EPS).T
            attn_low = attention(qkv, norms, gain_query, gain_key, cos_tab, sin_tab, mask)
            state = scatter_begin(net, lambda rows: contract_cols(attn_low[rows], out_w), n_tokens)
            return attn_low, norms, state

        out = region(flag, part_attend)
        own_up, far_gate, got_down, (attn_low, norms, state) = meet(own_up, far_gate, got_down, out)
        near_gate = spread(net, far_gate)
        block_down = both_rows([w_down], got_down)
        far_down = ahead(block_down)

        def part_resid():
            attn_sum = scatter_end(scatter_third(net, scatter_second(net, state)))
            norm_attn = lax.rsqrt(jnp.mean(attn_sum * attn_sum, -1, keepdims=True) + EPS)
            attn_hat = attn_sum * norm_attn
            resid = x_low.astype(F32) + attn_hat * gain_attn
            return norm_attn, attn_hat, resid, gather_begin(net, resid.astype(BF16))

        out = region(flag, part_resid)
        near_gate, far_up, (norm_attn, attn_hat, resid, state) = meet(near_gate, far_up, out)
        relay_up = spread(net, beyond(far_up))[1:]
        own_down = spread(net, block_down)[1:]

        def part_middle():
            return jnp.concatenate(gather_middle(net, state)[0], 0)

        mlp_mine = region(flag, part_middle)
        far_down, relay_up, mlp_mine = meet(far_down, relay_up, mlp_mine)
        relay_down = spread(net, beyond(far_down))[1:]

        def part_gate():
            mlp_in, _ = gather_cores(net, mlp_mine)
            return mlp_in, by_rows(mlp_in, near_gate)

        out = region(flag, part_gate)
        own_down, (mlp_in, gate_proj) = meet(own_down, out)

        def part_up():
            near_up = [far_up, *(in_two(own, other) for own, other in zip(own_up, relay_up))]
            up_proj = by_rows(mlp_in, near_up)
            hidden_act = (gate_proj * jax.nn.sigmoid(gate_proj) * up_proj).astype(BF16)
            return up_proj, hidden_act, near_up

        out = region(flag, part_up)
        relay_down, (up_proj, hidden_act, near_up) = meet(relay_down, out)

        act_halves = slice(hidden_act.shape[1] // 2), slice(hidden_act.shape[1] // 2, None)

        def part_down():
            down_w = stack(far_down, *(in_two(own, other) for own, other in zip(own_down, relay_down)))
            state = scatter_begin(net, lambda rows: contract_cols(hidden_act[rows], down_w), n_tokens)
            mlp_sum = scatter_end(scatter_third(net, scatter_second(net, state)))
            norm_mlp = lax.rsqrt(jnp.mean(mlp_sum * mlp_sum, -1, keepdims=True) + EPS)
            mlp_hat = mlp_sum * norm_mlp
            scaled = grad_out * gain_mlp
            grad_mlp = norm_mlp * (scaled - mlp_hat * jnp.mean(mlp_hat * scaled, -1, keepdims=True))
            grad_mlp_all, _ = gather_end(net, gather_middle(net, gather_begin(net, grad_mlp.astype(BF16))))
            seq = Sequence()
            sends = weight_grad(seq, grad_mlp_all, hidden_act, sent_pieces, act_halves[0])
            return down_w, mlp_hat, grad_mlp_all, sends, stack(*near_gate), stack(*near_up)

        down_w, mlp_hat, grad_mlp_all, sends, gate_w, up_w = region(flag, part_down)
        got_first = begin(net, sends)

        def part_back_act():
            seq = Sequence()
            keeps_first = weight_grad(seq, grad_mlp_all, hidden_act, kept_pieces, act_halves[0])

            def back_act(grad_mlp_all, down_w):
                sig_gate = jax.nn.sigmoid(gate_proj)
                grad_act = dot_rows_cols(grad_mlp_all, down_w)
                grad_gate = (grad_act * up_proj * (sig_gate * (1.0 + gate_proj * (1.0 - sig_gate)))).astype(BF16)
                return grad_gate, (grad_act * (gate_proj * sig_gate)).astype(BF16)

            grad_gate, grad_up = seq.run(back_act, grad_mlp_all, down_w)
            down_sends = weight_grad(seq, grad_mlp_all, hidden_act, sent_pieces, act_halves[1])
            gate_sends = weight_grad(seq, mlp_in, grad_gate, sent_pieces)
            return keeps_first, grad_gate, grad_up, down_sends, gate_sends

        out = region(flag, part_back_act)
        got_first, (keeps_first, grad_gate, grad_up, down_sends, gate_sends) = meet(got_first, out)
        got_second, got_gate = begin(net, down_sends), begin(net, gate_sends)
        down_first = behind(finish(net, keeps_first, got_first))

        def part_back_resid():
            seq = Sequence()
            state = scatter_begin(
                net,
                lambda rows: seq.run(
                    lambda a, b, c, d: contract_cols(a[rows], c) + contract_cols(b[rows], d),
                    grad_gate,
                    grad_up,
                    gate_w,
                    up_w,
                ),
                n_tokens,
            )
            return weight_grad(seq, grad_mlp_all, hidden_act, kept_pieces, act_halves[1]), state

        out = region(flag, part_back_resid)
        got_second, (keeps_second, state) = meet(got_second, out)
        down_second = behind(finish(net, keeps_second, got_second))

        def part_back_attn():
            seq = Sequence()
            later = scatter_second(net, state)
            keeps_gate = weight_grad(seq, mlp_in, grad_gate, kept_pieces)
            seq.wait(*later[2])
            later = scatter_third(net, later)
            sends = weight_grad(seq, mlp_in, grad_up, sent_pieces)
            seq.wait(*later[2])
            grad_resid = grad_out + scatter_end(later)
            scaled = grad_resid * gain_attn
            grad_attn = norm_attn * (scaled - attn_hat * jnp.mean(attn_hat * scaled, -1, keepdims=True))
            first = gather_begin(net, grad_attn.astype(BF16))
            gain_row_attn = jnp.sum(grad_resid * attn_hat, 0, keepdims=True)
            keeps_up = weight_grad(seq, mlp_in, grad_up, kept_pieces)
            return keeps_gate, sends, keeps_up, grad_resid, first, gain_row_attn

        out = region(flag, part_back_attn)
        got_gate, down_first, out = meet(got_gate, down_first, out)
        keeps_gate, sends, keeps_up, grad_resid, state, gain_row_attn = out
        got_up = begin(net, sends)
        total_gate = behind(finish(net, keeps_gate, got_gate))

        def part_back_heads():
            grad_attn_all, _ = gather_end(net, gather_middle(net, state))
            grad_heads = dot_rows_cols(grad_attn_all, out_w).astype(BF16)
            return grad_attn_all, attention(qkv, norms, gain_query, gain_key, cos_tab, sin_tab, mask, grad_heads)

        out = region(flag, part_back_heads)
        got_up, down_second, (grad_attn_all, grads) = meet(got_up, down_second, out)
        grad_query_n, grad_key_n, grad_value_low, inner_parts, head_gains = grads
        total_up = behind(finish(net, keeps_up, got_up))

        def part_back_value():
            seq = Sequence()
            inner, received = add_stats(net, jnp.sum(inner_parts, 0).reshape(n_tokens, 2).T)
            sends = [
                jnp.concatenate(pair, 1)
                for pair in zip(
                    weight_grad(seq, x_all, grad_value_low, sent_pieces),
                    weight_grad(seq, grad_attn_all, attn_low, sent_pieces),
                )
            ]
            total_down = jnp.concatenate([down_first, down_second], 1)
            return inner, sends, total_down, to_leave(total_down)

        inner, sends, total_down, leave = region(flag, part_back_value)
        got_first, got_down = begin(net, sends), net.send(leave, col)

        def part_back_qkv():
            seq = Sequence()
            qkv_w = stack(*(part[:, qkv_cols] for part in near_attn))
            keeps_first = [
                jnp.concatenate(pair, 1)
                for pair in zip(
                    weight_grad(seq, x_all, grad_value_low, kept_pieces),
                    weight_grad(seq, grad_attn_all, attn_low, kept_pieces),
                )
            ]
            scale = inner.T / model_width

            def through_norm(grad, i, gain):
                hat = qkv[:, i * head_cols : (i + 1) * head_cols] * norms[:, i : i + 1]
                return (norms[:, i : i + 1] * (grad * gain - hat * scale[:, i : i + 1])).astype(BF16)

            qk_right = seq.run(
                lambda a, b: jnp.concatenate(
                    [through_norm(a, 0, gain_query), through_norm(b, 1, gain_key)], 1
                ),
                grad_query_n,
                grad_key_n,
            )
            return qk_right, keeps_first, weight_grad(seq, x_all, qk_right, sent_pieces), qkv_w

        out = region(flag, part_back_qkv)
        got_first, total_gate, (qk_right, keeps_first, sends, qkv_w) = meet(got_first, total_gate, out)
        got_second = begin(net, sends)
        vo_total = behind(finish(net, keeps_first, got_first))
        got_gate = net.send(to_leave(total_gate), col)

        def part_in_part():
            keeps_second = weight_grad(Sequence(), x_all, qk_right, kept_pieces)
            qkv_right = jnp.concatenate([qk_right, grad_value_low], 1)
            head_rows = lax.dynamic_update_slice(
                jnp.zeros((2, model_width), F32), head_gains, (jnp.int32(0), offset)
            )
            gain_row_mlp = jnp.sum(grad_out * mlp_hat, 0, keepdims=True)
            post_rows = lay.from_relative(jnp.concatenate([gain_row_attn, gain_row_mlp], 0))
            gain_rows = add_all(net, jnp.concatenate([head_rows, post_rows], 0), (side, core))
            return keeps_second, scatter_begin(net, lambda rows: contract_cols(qkv_right[rows], qkv_w), n_tokens), gain_rows

        out = region(flag, part_in_part)
        got_second, got_down, got_gate, total_up, out = meet(got_second, got_down, got_gate, total_up, out)
        keeps_second, state, gain_rows = out
        got_up = net.send(to_leave(total_up), col)
        qk_total = behind(finish(net, keeps_second, got_second))

        def part_outputs():
            ending = scatter_third(net, scatter_second(net, state))
            gate_grad = jnp.concatenate(owned(total_gate, got_gate), 1)
            down_grad = jnp.concatenate(owned(total_down, got_down), 1)
            hidden_out = lay.from_relative((resid + mlp_hat * gain_mlp).astype(BF16))
            near_rows = add_all(net, gain_rows, lay.near)
            return ending, gate_grad, down_grad, hidden_out, near_rows

        out = region(flag, part_outputs)
        vo_total, qk_total, got_up, out = meet(vo_total, qk_total, got_up, out)
        state, gate_grad, down_grad, hidden_out, gain_rows = out
        got_vo, got_qk = net.send(to_leave(vo_total), col), net.send(to_leave(qk_total), col)

        def part_last():
            gains_grad = add_all(net, gain_rows, (lay.far, lay.col_axis))
            up_grad = jnp.concatenate(owned(total_up, got_up), 1)
            return lay.from_relative(grad_resid + scatter_end(state)), up_grad, gains_grad

        out = region(flag, part_last)
        got_vo, got_qk, (in_grad, up_grad, gains_grad) = meet(got_vo, got_qk, out)
        vo_pair = owned(vo_total, got_vo)
        qk_pair = owned(qk_total, got_qk)
        query_grad, key_grad, value_grad, out_grad_own = (
            jnp.concatenate([part[:, i * head_cols : (i + 1) * head_cols] for part in pair], 1)
            for pair in (qk_pair, vo_pair)
            for i in range(2)
        )
        return (
            hidden_out,
            in_grad,
            query_grad,
            key_grad,
            value_grad,
            out_grad_own,
            gate_grad,
            up_grad,
            down_grad,
            gains_grad,
        )

    return on_device


def solution(mesh):
    lay = Layout(mesh.shape["dp"], mesh.shape["tensor"])
    fine = Mesh(mesh.devices.reshape(lay.shape_of()), lay.dp_axes + lay.tensor_axes)
    tokens = P(lay.dp_axes + lay.tensor_axes, None)
    weights = P(lay.dp_axes, lay.tensor_axes)
    rows = P(lay.dp_axes)
    return jax.shard_map(
        block_program(lay),
        mesh=fine,
        in_specs=(tokens, tokens) + (weights,) * 7 + (P(), rows, rows),
        out_specs=(tokens, tokens) + (weights,) * 7 + (P(),),
        check_vma=False,
    )
```

```python
import jax
import jax.numpy as jnp
from jax import lax
from jax.experimental import pallas as pl
from jax.experimental.pallas import tpu as pltpu
from jax.experimental.layout import Layout as Order, with_layout_constraint
from jax.sharding import Mesh, PartitionSpec as P

HEAD_DIM = 128
EPS = 1e-06
THETA = 500000.0
NEG = -1e30
F32 = jnp.float32
BF16 = jnp.bfloat16


def dot_rows_cols(left, right):
    return jnp.dot(left, right, preferred_element_type=F32)


def contract_cols(left, right):
    return lax.dot_general(left, right, (((1,), (1,)), ((), ())), preferred_element_type=F32)


def contract_rows(left, right):
    return lax.dot_general(left, right, (((0,), (0,)), ((), ())), preferred_element_type=F32)


def swap(values, axis):
    return lax.ppermute(values, axis, [(0, 1), (1, 0)])


def pick(flag, yes, no):
    return jnp.where(flag, yes, no)


def after(values, *done):
    return lax.optimization_barrier((values,) + done)[0] if done else values


class Net:
    def send(self, values, axis):
        return swap(values, axis)


def region(flag, step):
    out = jax.eval_shape(step)
    return lax.cond(flag, step, lambda: jax.tree.map(lambda leaf: jnp.zeros(leaf.shape, leaf.dtype), out))


def meet(*values):
    leaves, tree = jax.tree.flatten(values)
    return jax.tree.unflatten(tree, lax.optimization_barrier(tuple(leaves)))


class Sequence:
    def __init__(self):
        self.done = ()

    def wait(self, *received):
        self.done = self.done + received

    def run(self, step, *operands):
        if self.done:
            operands = lax.optimization_barrier(operands + self.done)[: len(operands)]
        out = step(*operands)
        self.done = out if isinstance(out, tuple) else (out,)
        return out


class Layout:
    def __init__(self, n_dp, n_tensor):
        self.dp_axes = tuple(f"d{i}" for i in range(n_dp.bit_length() - 1))
        self.tensor_axes = tuple(f"t{i}" for i in range(n_tensor.bit_length() - 1))
        self.col_axis = self.dp_axes[1]
        self.far = self.dp_axes[0]
        self.near = tuple(a for a in self.dp_axes if a not in (self.far, self.col_axis))
        self.core, self.side = self.tensor_axes[1], self.tensor_axes[0]
        self.n_dp = n_dp
        self.n_bits = len(self.dp_axes)

    def shape_of(self):
        return (2,) * (len(self.dp_axes) + len(self.tensor_axes))

    def dp_mask(self, axis):
        return 1 << (self.n_bits - 1 - self.dp_axes.index(axis))

    def block_order(self):
        order = []
        for j in range(1 << len(self.near)):
            block = sum(self.dp_mask(axis) for i, axis in enumerate(self.near) if (j >> i) & 1)
            for ahead in (0, self.dp_mask(self.far)):
                order += [block | ahead, block | ahead | self.dp_mask(self.col_axis)]
        return order

    def flip_blocks(self, blocks):
        for axis in self.near:
            flag, mask = lax.axis_index(axis) == 1, self.dp_mask(axis)
            blocks = [pick(flag, blocks[b ^ mask], blocks[b]) for b in range(len(blocks))]
        return blocks

    def to_relative(self, values):
        width = values.shape[-1] // self.n_dp
        blocks = [values[..., b * width : (b + 1) * width] for b in range(self.n_dp)]
        blocks = self.flip_blocks(blocks)
        return jnp.concatenate([blocks[b] for b in self.block_order()], -1)

    def from_relative(self, values):
        width = values.shape[-1] // self.n_dp
        blocks = [None] * self.n_dp
        for place, b in enumerate(self.block_order()):
            blocks[b] = values[..., place * width : (place + 1) * width]
        return jnp.concatenate(self.flip_blocks(blocks), -1)


def rope_tables(pos_col):
    lane = jnp.arange(HEAD_DIM, dtype=jnp.int32)[None, :]
    pair = (lane % (HEAD_DIM // 2)).astype(F32)
    inverse = THETA ** (-(pair * 2.0 / HEAD_DIM))
    angles = pos_col.astype(F32) * inverse
    return jnp.cos(angles), jnp.sin(angles) * jnp.where(lane < HEAD_DIM // 2, -1.0, 1.0)


def load_rows(ref):
    values = ref[...]
    return values.reshape(-1, values.shape[-1])


def head_scores(q_ref, k_ref, norm_ref, gain_q_ref, gain_k_ref, cos_ref, sin_ref, mask_ref):
    norms, cos_tab, sin_tab = load_rows(norm_ref), load_rows(cos_ref), load_rows(sin_ref)

    def rotated(values, gain):
        values = values * gain
        return (values * cos_tab + pltpu.roll(values, HEAD_DIM // 2, 1) * sin_tab).astype(BF16)

    query_hat = load_rows(q_ref) * norms[:, 0:1]
    key_hat = load_rows(k_ref) * norms[:, 1:2]
    q_rot = rotated(query_hat, gain_q_ref[...])
    k_rot = rotated(key_hat, gain_k_ref[...])
    scores = contract_cols(q_rot, k_rot) * HEAD_DIM ** (-0.5)
    scores = jnp.where(mask_ref[0] > 0, scores, NEG)
    exp_scores = jnp.exp(scores - jnp.max(scores, -1, keepdims=True))
    probs = exp_scores / jnp.sum(exp_scores, -1, keepdims=True)
    return query_hat, key_hat, q_rot, k_rot, probs, cos_tab, sin_tab


def attend_kernel(q_ref, k_ref, v_ref, norm_ref, gain_q_ref, gain_k_ref, cos_ref, sin_ref, mask_ref, out_ref):
    probs = head_scores(q_ref, k_ref, norm_ref, gain_q_ref, gain_k_ref, cos_ref, sin_ref, mask_ref)[4]
    out = dot_rows_cols(probs.astype(BF16), load_rows(v_ref).astype(BF16)).astype(BF16)
    out_ref[...] = out.reshape(out_ref.shape)


def attend_back_kernel(
    q_ref, k_ref, v_ref, norm_ref, gain_q_ref, gain_k_ref, cos_ref, sin_ref, mask_ref, grad_ref,
    grad_q_ref, grad_k_ref, grad_v_ref, inner_ref, gains_ref,
):
    query_hat, key_hat, q_rot, k_rot, probs, cos_tab, sin_tab = head_scores(
        q_ref, k_ref, norm_ref, gain_q_ref, gain_k_ref, cos_ref, sin_ref, mask_ref
    )
    grad_head = load_rows(grad_ref)
    grad_prob = contract_cols(grad_head, load_rows(v_ref).astype(BF16))
    row_dot = jnp.sum(probs * grad_prob, -1, keepdims=True)
    grad_scores = (probs * (grad_prob - row_dot)).astype(BF16)
    scale = HEAD_DIM ** (-0.5)

    def unrotated(values):
        return values * cos_tab - pltpu.roll(values, HEAD_DIM // 2, 1) * sin_tab

    grad_q = unrotated(dot_rows_cols(grad_scores, k_rot) * scale)
    grad_k = unrotated(contract_rows(grad_scores, q_rot) * scale)
    grad_v = contract_rows(probs.astype(BF16), grad_head).astype(BF16)
    product_q, product_k = grad_q * query_hat, grad_k * key_hat
    inner_q = jnp.sum(product_q * gain_q_ref[...], -1, keepdims=True)
    inner_k = jnp.sum(product_k * gain_k_ref[...], -1, keepdims=True)
    grad_q_ref[...] = grad_q.reshape(grad_q_ref.shape)
    grad_k_ref[...] = grad_k.reshape(grad_k_ref.shape)
    grad_v_ref[...] = grad_v.reshape(grad_v_ref.shape)
    inner_ref[...] = jnp.concatenate([inner_q, inner_k], 1).reshape(inner_ref.shape)
    gains_ref[...] = jnp.concatenate(
        [jnp.sum(product_q, 0, keepdims=True), jnp.sum(product_k, 0, keepdims=True)], 0
    ).reshape(gains_ref.shape)


def attention(qkv, norms, gain_query, gain_key, cos_tab, sin_tab, mask, grad_heads=None):
    n_tokens = qkv.shape[0]
    rows, n_heads = n_tokens // 4, qkv.shape[1] // (3 * HEAD_DIM)

    def split(values):
        return values.reshape(2, 2, rows, values.shape[-1])

    def columns(first):
        return pl.BlockSpec((2, 1, rows, HEAD_DIM), lambda s, h: (0, s, 0, first + h))

    def whole(width):
        return pl.BlockSpec((2, 1, rows, width), lambda s, h: (0, s, 0, 0))

    gain = pl.BlockSpec((1, HEAD_DIM), lambda s, h: (0, h))
    in_specs = [columns(0), columns(n_heads), columns(2 * n_heads), whole(2), gain, gain, whole(HEAD_DIM), whole(HEAD_DIM)]
    in_specs.append(pl.BlockSpec((1, 2 * rows, 2 * rows), lambda s, h: (s, 0, 0)))
    heads = split(qkv)
    operands = [heads, heads, heads, split(norms), gain_query[None], gain_key[None], split(cos_tab), split(sin_tab), mask]
    shape = (2, 2, rows, n_heads * HEAD_DIM)
    kernel, out_specs, out_shape = attend_kernel, columns(0), jax.ShapeDtypeStruct(shape, BF16)
    if grad_heads is not None:
        in_specs.append(columns(0))
        operands.append(split(grad_heads))
        kernel = attend_back_kernel
        out_specs = (
            columns(0),
            columns(0),
            columns(0),
            pl.BlockSpec((1, 2, 1, rows, 2), lambda s, h: (h, 0, s, 0, 0)),
            pl.BlockSpec((1, 2, HEAD_DIM), lambda s, h: (s, 0, h)),
        )
        out_shape = (
            jax.ShapeDtypeStruct(shape, F32),
            jax.ShapeDtypeStruct(shape, F32),
            jax.ShapeDtypeStruct(shape, BF16),
            jax.ShapeDtypeStruct((n_heads, 2, 2, rows, 2), F32),
            jax.ShapeDtypeStruct((2, 2, n_heads * HEAD_DIM), F32),
        )
    out = pl.pallas_call(
        kernel,
        grid=(2, n_heads),
        in_specs=in_specs,
        out_specs=out_specs,
        out_shape=out_shape,
        compiler_params=pltpu.CompilerParams(vmem_limit_bytes=48 * 1024 * 1024),
        cost_estimate=pl.CostEstimate(flops=1 << 30, bytes_accessed=1 << 23, transcendentals=1 << 20),
    )(*operands)
    if grad_heads is None:
        return out.reshape(n_tokens, -1)
    return tuple(part.reshape(n_tokens, -1) for part in out[:3]) + (out[3], jnp.sum(out[4], 0))


def block_program(lay):
    col, side, core = lay.col_axis, lay.side, lay.core

    def my(axis):
        return lax.axis_index(axis)

    def halves(weights):
        half = [w.shape[1] // 2 for w in weights]
        low = jnp.concatenate([w[:, :h] for w, h in zip(weights, half)], 1)
        high = jnp.concatenate([w[:, h:] for w, h in zip(weights, half)], 1)
        return low, high

    def leaving(weights):
        low, high = halves(weights)
        return pick(my(col) == 0, high, low)

    def both_rows(weights, got):
        low, high = halves(weights)
        first = my(col) == 0
        return jnp.concatenate([pick(first, low, got), pick(first, got, high)], 0)

    def ahead(block):
        return lax.all_gather(block, lay.far, axis=0, tiled=True)

    def beyond(both):
        half = both.shape[0] // 2
        return lax.dynamic_slice_in_dim(both, (1 - my(lay.far)) * half, half, 0)

    def in_two(own, other):
        first = my(lay.far) == 0
        return jnp.concatenate([pick(first, own, other), pick(first, other, own)], 0)

    def behind(total):
        return lax.psum_scatter(total.astype(BF16), lay.far, scatter_dimension=0, tiled=True)

    def spread(net, block):
        pieces = [block]
        for axis in lay.near:
            pieces = pieces + [net.send(piece, axis) for piece in pieces]
        return pieces

    def begin(net, grads):
        return [net.send(grad, lay.near[-1]) for grad in grads]

    def finish(net, keeps, received):
        pieces = [a.astype(F32) + b.astype(F32) for a, b in zip(keeps, received)]
        for axis in reversed(lay.near[:-1]):
            half = len(pieces) // 2
            others = [net.send(piece.astype(BF16), axis) for piece in pieces[half:]]
            pieces = [a + b.astype(F32) for a, b in zip(pieces[:half], others)]
        return pieces[0].astype(BF16)

    def to_leave(total):
        half = total.shape[0] // 2
        return pick(my(col) == 0, total[half:], total[:half]).astype(BF16)

    def owned(total, got):
        half = total.shape[0] // 2
        first = my(col) == 0
        mine, got = pick(first, total[:half], total[half:]), got.astype(F32)
        return pick(first, mine, got), pick(first, got, mine)

    def gather_begin(net, own):
        half = own.shape[0] // 2
        a0, b0 = own[:half], own[half:]
        return a0, b0, net.send(a0, side), net.send(b0, col)

    def gather_middle(net, state):
        a0, b0, a_side, b_col = state
        half = a0.shape[0]
        a_far = net.send(jnp.concatenate([a0, a_side], 0), col)
        b_far = net.send(jnp.concatenate([b0, b_col], 0), side)
        return [a0, b0, a_side, b_far[:half], a_far[:half], b_col, a_far[half:], b_far[half:]], (a_far, b_far)

    def gather_end(net, state):
        mine = jnp.concatenate(state[0], 0)
        other = net.send(mine, core)
        return jnp.concatenate([mine, other], 0), other

    def scatter_begin(net, product, n_rows):
        half = n_rows // 2
        received = net.send(product(slice(half, None)).astype(BF16), core)
        return product(slice(half)).astype(BF16), received

    def scatter_second(net, state):
        part = state[0].astype(F32) + state[1].astype(F32)
        half = part.shape[0] // 8
        a0, b0, a_side, b_side, a_col, b_col, a_both, b_both = (part[i * half : (i + 1) * half] for i in range(8))
        received = (
            net.send(jnp.concatenate([a_col, a_both], 0).astype(BF16), col),
            net.send(jnp.concatenate([b_side, b_both], 0).astype(BF16), side),
        )
        return jnp.concatenate([a0, a_side], 0), jnp.concatenate([b0, b_col], 0), received

    def scatter_third(net, state):
        a_sum, b_sum = (own + got.astype(F32) for own, got in zip(state[:2], state[2]))
        half = a_sum.shape[0] // 2
        received = net.send(a_sum[half:].astype(BF16), side), net.send(b_sum[half:].astype(BF16), col)
        return a_sum[:half], b_sum[:half], received

    def scatter_end(state):
        a0, b0, received = state
        return jnp.concatenate([a0 + received[0].astype(F32), b0 + received[1].astype(F32)], 0)

    def token_rows(values, exchange):
        quarters = values.reshape(4, -1)
        rows = [quarters[0:1], quarters[1:2], quarters[2:3], quarters[3:4]]
        for axis, mask in ((side, 2), (core, 1)):
            flag = my(axis) == 1
            rows = [pick(flag, rows[i ^ mask], rows[i]) for i in range(4)]
        own = jnp.concatenate(rows, 0)
        other = exchange(own)
        order = [own[0:1], own[2:3], other[0:1], other[2:3], own[1:2], own[3:4], other[1:2], other[3:4]]
        return jnp.concatenate(order, 0)

    def token_rows_of(positions, seg_ids, net):
        rows = []

        def exchange(own):
            rows.append(own)
            return own

        token_rows(positions, exchange)
        token_rows(seg_ids, exchange)
        other = net.send(jnp.concatenate(rows, 0), col)
        return [
            token_rows(values, lambda own, i=i: other[4 * i : 4 * i + 4])
            for i, values in enumerate((positions, seg_ids))
        ]

    def add_all(net, values, axes):
        for axis in axes:
            received = net.send(values, axis)
            values = values + received
        return values

    def add_stats(net, rows):
        rows = rows.reshape(-1, 2, 2, 2, rows.shape[1] // 8)
        for dim, axis in ((1, core), (2, col), (3, side)):
            received = net.send(rows, axis)
            rows = rows + jnp.flip(received, dim)
        return rows.reshape(rows.shape[0], -1), received

    def on_device(
        hidden_in, out_grad, w_query, w_key, w_value, w_out, w_gate, w_up, w_down, gains, seg_ids, positions
    ):
        model_width = hidden_in.shape[1]
        head_cols = w_query.shape[1] // 2
        n_heads = head_cols // HEAD_DIM
        n_tokens = hidden_in.shape[0] * 8
        seq_len = n_tokens // 2
        score_scale = HEAD_DIM ** (-0.5)
        place = my(side) * 4 + my(core) * 2 + my(col)
        offset = place * head_cols
        per = seq_len // 4

        def by_seq(rows):
            return rows.reshape(2, 2, 2 * per).transpose(1, 0, 2).reshape(2, seq_len)

        net = Net()
        flag = positions[0] >= 0
        n_near = 1 << len(lay.near)
        piece = model_width // n_near
        kept_pieces, sent_pieces = range(n_near // 2), range(n_near // 2, n_near)

        def stack(*parts):
            return jnp.concatenate(parts, 0)

        def by_rows(left, pieces, cols=slice(None)):
            return sum(
                dot_rows_cols(left[:, j * piece : (j + 1) * piece], block[:, cols]) for j, block in enumerate(pieces)
            )

        def weight_grad(seq, left, right, which, cols=slice(None)):
            return [
                seq.run(
                    lambda a, b, j=j: contract_rows(a[:, j * piece : (j + 1) * piece], b[:, cols]).astype(BF16),
                    left,
                    right,
                )
                for j in which
            ]

        attn_weights = [w_query, w_key, w_value, w_out]

        def part_first():
            block_attn = both_rows(attn_weights, net.send(leaving(attn_weights), col))
            return block_attn, leaving([w_gate]), leaving([w_up]), lay.to_relative(hidden_in)

        block_attn, leave_gate, leave_up, x_low = region(flag, part_first)
        far_attn, own_attn = ahead(block_attn), spread(net, block_attn)[1:]

        def part_tokens():
            state = gather_begin(net, x_low)
            got_gate = net.send(after(leave_gate, *state[2:]), col)
            state = gather_middle(net, (*state[:3], after(state[3], got_gate)))
            tables = token_rows_of(positions, seg_ids, net)
            return state, leaving([w_down]), both_rows([w_gate], got_gate), tables

        out = region(flag, part_tokens)
        far_attn, own_attn, (state, leave_down, block_gate, (pos_rows, seg_rows)) = meet(far_attn, own_attn, out)
        got_up = net.send(leave_up, col)
        relay_attn = spread(net, beyond(far_attn))[1:]
        far_gate = ahead(block_gate)

        def part_tables():
            x_all, _ = gather_end(net, state)
            cos_tab, sin_tab = rope_tables(pos_rows.reshape(n_tokens, 1))
            ids_rows = token_rows(jnp.arange(seq_len, dtype=jnp.int32), lambda rows: rows)
            seg_seq, ids_seq = by_seq(seg_rows), by_seq(ids_rows)
            mask = (seg_seq[:, :, None] == seg_seq[:, None, :]) & (ids_seq[:, :, None] >= ids_seq[:, None, :])
            mask = mask.astype(F32)
            gain_query = lax.dynamic_slice_in_dim(gains[0], offset, head_cols)
            gain_key = lax.dynamic_slice_in_dim(gains[1], offset, head_cols)
            gain_post = lay.to_relative(gains[2:4])
            more = gain_query, gain_key, gain_post[0:1], gain_post[1:2], lay.to_relative(out_grad).astype(F32)
            return x_all, cos_tab, sin_tab, mask, more

        out = region(flag, part_tables)
        relay_attn, got_up, (x_all, cos_tab, sin_tab, mask, more) = meet(relay_attn, got_up, out)
        gain_query, gain_key, gain_attn, gain_mlp, grad_out = more
        block_up = both_rows([w_up], got_up)
        far_up, own_up = ahead(block_up), spread(net, block_up)[1:]
        qkv_cols, out_cols = slice(3 * head_cols), slice(3 * head_cols, None)


        def part_qkv():
            near_attn = [far_attn, *(in_two(own, other) for own, other in zip(own_attn, relay_attn))]
            qkv = with_layout_constraint(by_rows(x_all, near_attn, qkv_cols), Order((0, 1)))
            squares, _ = add_stats(
                net,
                jnp.stack(
                    [jnp.sum(part * part, -1) for part in (qkv[:, :head_cols], qkv[:, head_cols : 2 * head_cols])], 0
                ),
            )
            return near_attn, qkv, squares, stack(*(block[:, out_cols] for block in near_attn))

        out = region(flag, part_qkv)
        leave_down, (near_attn, qkv, squares, out_w) = meet(leave_down, out)
        got_down = net.send(leave_down, col)

        def part_attend():
            norms = lax.rsqrt(squares / model_width + EPS).T
            attn_low = attention(qkv, norms, gain_query, gain_key, cos_tab, sin_tab, mask)
            state = scatter_begin(net, lambda rows: contract_cols(attn_low[rows], out_w), n_tokens)
            return attn_low, norms, state

        out = region(flag, part_attend)
        own_up, far_gate, got_down, (attn_low, norms, state) = meet(own_up, far_gate, got_down, out)
        near_gate = spread(net, far_gate)
        block_down = both_rows([w_down], got_down)
        far_down = ahead(block_down)

        def part_resid():
            attn_sum = scatter_end(scatter_third(net, scatter_second(net, state)))
            norm_attn = lax.rsqrt(jnp.mean(attn_sum * attn_sum, -1, keepdims=True) + EPS)
            attn_hat = attn_sum * norm_attn
            resid = x_low.astype(F32) + attn_hat * gain_attn
            return norm_attn, attn_hat, resid, gather_begin(net, resid.astype(BF16))

        out = region(flag, part_resid)
        near_gate, far_up, (norm_attn, attn_hat, resid, state) = meet(near_gate, far_up, out)
        relay_up = spread(net, beyond(far_up))[1:]
        own_down = spread(net, block_down)[1:]

        def part_gate():
            mlp_in, _ = gather_end(net, gather_middle(net, state))
            return mlp_in, by_rows(mlp_in, near_gate)

        out = region(flag, part_gate)
        relay_up, own_down, far_down, (mlp_in, gate_proj) = meet(relay_up, own_down, far_down, out)
        relay_down = spread(net, beyond(far_down))[1:]

        def part_up():
            near_up = [far_up, *(in_two(own, other) for own, other in zip(own_up, relay_up))]
            up_proj = by_rows(mlp_in, near_up)
            hidden_act = (gate_proj * jax.nn.sigmoid(gate_proj) * up_proj).astype(BF16)
            return up_proj, hidden_act, near_up

        out = region(flag, part_up)
        relay_down, (up_proj, hidden_act, near_up) = meet(relay_down, out)

        act_halves = slice(hidden_act.shape[1] // 2), slice(hidden_act.shape[1] // 2, None)

        def part_down():
            down_w = stack(far_down, *(in_two(own, other) for own, other in zip(own_down, relay_down)))
            state = scatter_begin(net, lambda rows: contract_cols(hidden_act[rows], down_w), n_tokens)
            mlp_sum = scatter_end(scatter_third(net, scatter_second(net, state)))
            norm_mlp = lax.rsqrt(jnp.mean(mlp_sum * mlp_sum, -1, keepdims=True) + EPS)
            mlp_hat = mlp_sum * norm_mlp
            scaled = grad_out * gain_mlp
            grad_mlp = norm_mlp * (scaled - mlp_hat * jnp.mean(mlp_hat * scaled, -1, keepdims=True))
            grad_mlp_all, _ = gather_end(net, gather_middle(net, gather_begin(net, grad_mlp.astype(BF16))))
            seq = Sequence()
            sends = weight_grad(seq, grad_mlp_all, hidden_act, sent_pieces, act_halves[0])
            return down_w, mlp_hat, grad_mlp_all, sends, stack(*near_gate), stack(*near_up)

        down_w, mlp_hat, grad_mlp_all, sends, gate_w, up_w = region(flag, part_down)
        got_first = begin(net, sends)

        def part_back_act():
            seq = Sequence()
            keeps_first = weight_grad(seq, grad_mlp_all, hidden_act, kept_pieces, act_halves[0])

            def back_act(grad_mlp_all, down_w):
                sig_gate = jax.nn.sigmoid(gate_proj)
                grad_act = dot_rows_cols(grad_mlp_all, down_w)
                grad_gate = (grad_act * up_proj * (sig_gate * (1.0 + gate_proj * (1.0 - sig_gate)))).astype(BF16)
                return grad_gate, (grad_act * (gate_proj * sig_gate)).astype(BF16)

            grad_gate, grad_up = seq.run(back_act, grad_mlp_all, down_w)
            down_sends = weight_grad(seq, grad_mlp_all, hidden_act, sent_pieces, act_halves[1])
            gate_sends = weight_grad(seq, mlp_in, grad_gate, sent_pieces)
            return keeps_first, grad_gate, grad_up, down_sends, gate_sends

        out = region(flag, part_back_act)
        got_first, (keeps_first, grad_gate, grad_up, down_sends, gate_sends) = meet(got_first, out)
        got_second, got_gate = begin(net, down_sends), begin(net, gate_sends)
        down_first = behind(finish(net, keeps_first, got_first))

        def part_back_resid():
            seq = Sequence()
            state = scatter_begin(
                net,
                lambda rows: seq.run(
                    lambda a, b, c, d: contract_cols(a[rows], c) + contract_cols(b[rows], d),
                    grad_gate,
                    grad_up,
                    gate_w,
                    up_w,
                ),
                n_tokens,
            )
            return weight_grad(seq, grad_mlp_all, hidden_act, kept_pieces, act_halves[1]), state

        out = region(flag, part_back_resid)
        got_second, (keeps_second, state) = meet(got_second, out)
        down_second = behind(finish(net, keeps_second, got_second))

        def part_back_attn():
            seq = Sequence()
            later = scatter_second(net, state)
            keeps_gate = weight_grad(seq, mlp_in, grad_gate, kept_pieces)
            seq.wait(*later[2])
            later = scatter_third(net, later)
            sends = weight_grad(seq, mlp_in, grad_up, sent_pieces)
            seq.wait(*later[2])
            grad_resid = grad_out + scatter_end(later)
            scaled = grad_resid * gain_attn
            grad_attn = norm_attn * (scaled - attn_hat * jnp.mean(attn_hat * scaled, -1, keepdims=True))
            first = gather_begin(net, grad_attn.astype(BF16))
            gain_row_attn = jnp.sum(grad_resid * attn_hat, 0, keepdims=True)
            keeps_up = weight_grad(seq, mlp_in, grad_up, kept_pieces)
            return keeps_gate, sends, keeps_up, grad_resid, first, gain_row_attn

        out = region(flag, part_back_attn)
        got_gate, down_first, out = meet(got_gate, down_first, out)
        keeps_gate, sends, keeps_up, grad_resid, state, gain_row_attn = out
        got_up = begin(net, sends)
        total_gate = behind(finish(net, keeps_gate, got_gate))

        def part_back_heads():
            grad_attn_all, _ = gather_end(net, gather_middle(net, state))
            grad_heads = dot_rows_cols(grad_attn_all, out_w).astype(BF16)
            return grad_attn_all, attention(qkv, norms, gain_query, gain_key, cos_tab, sin_tab, mask, grad_heads)

        out = region(flag, part_back_heads)
        got_up, down_second, (grad_attn_all, grads) = meet(got_up, down_second, out)
        grad_query_n, grad_key_n, grad_value_low, inner_parts, head_gains = grads
        total_up = behind(finish(net, keeps_up, got_up))

        def part_back_value():
            seq = Sequence()
            inner, received = add_stats(net, jnp.sum(inner_parts, 0).reshape(n_tokens, 2).T)
            sends = [
                jnp.concatenate(pair, 1)
                for pair in zip(
                    weight_grad(seq, x_all, grad_value_low, sent_pieces),
                    weight_grad(seq, grad_attn_all, attn_low, sent_pieces),
                )
            ]
            total_down = jnp.concatenate([down_first, down_second], 1)
            return inner, sends, total_down, to_leave(total_down)

        inner, sends, total_down, leave = region(flag, part_back_value)
        got_first, got_down = begin(net, sends), net.send(leave, col)

        def part_back_qkv():
            seq = Sequence()
            qkv_w = stack(*(part[:, qkv_cols] for part in near_attn))
            keeps_first = [
                jnp.concatenate(pair, 1)
                for pair in zip(
                    weight_grad(seq, x_all, grad_value_low, kept_pieces),
                    weight_grad(seq, grad_attn_all, attn_low, kept_pieces),
                )
            ]
            scale = inner.T / model_width

            def through_norm(grad, i, gain):
                hat = qkv[:, i * head_cols : (i + 1) * head_cols] * norms[:, i : i + 1]
                return (norms[:, i : i + 1] * (grad * gain - hat * scale[:, i : i + 1])).astype(BF16)

            qk_right = seq.run(
                lambda a, b: jnp.concatenate(
                    [through_norm(a, 0, gain_query), through_norm(b, 1, gain_key)], 1
                ),
                grad_query_n,
                grad_key_n,
            )
            return qk_right, keeps_first, weight_grad(seq, x_all, qk_right, sent_pieces), qkv_w

        out = region(flag, part_back_qkv)
        got_first, total_gate, (qk_right, keeps_first, sends, qkv_w) = meet(got_first, total_gate, out)
        got_second = begin(net, sends)
        vo_total = behind(finish(net, keeps_first, got_first))
        got_gate = net.send(to_leave(total_gate), col)

        def part_in_part():
            keeps_second = weight_grad(Sequence(), x_all, qk_right, kept_pieces)
            qkv_right = jnp.concatenate([qk_right, grad_value_low], 1)
            head_rows = lax.dynamic_update_slice(
                jnp.zeros((2, model_width), F32), head_gains, (jnp.int32(0), offset)
            )
            gain_row_mlp = jnp.sum(grad_out * mlp_hat, 0, keepdims=True)
            post_rows = lay.from_relative(jnp.concatenate([gain_row_attn, gain_row_mlp], 0))
            gain_rows = add_all(net, jnp.concatenate([head_rows, post_rows], 0), (side, core))
            return keeps_second, scatter_begin(net, lambda rows: contract_cols(qkv_right[rows], qkv_w), n_tokens), gain_rows

        out = region(flag, part_in_part)
        got_second, got_down, got_gate, total_up, out = meet(got_second, got_down, got_gate, total_up, out)
        keeps_second, state, gain_rows = out
        got_up = net.send(to_leave(total_up), col)
        qk_total = behind(finish(net, keeps_second, got_second))

        def part_outputs():
            ending = scatter_third(net, scatter_second(net, state))
            gate_grad = jnp.concatenate(owned(total_gate, got_gate), 1)
            down_grad = jnp.concatenate(owned(total_down, got_down), 1)
            hidden_out = lay.from_relative((resid + mlp_hat * gain_mlp).astype(BF16))
            near_rows = add_all(net, gain_rows, lay.near)
            return ending, gate_grad, down_grad, hidden_out, near_rows

        out = region(flag, part_outputs)
        vo_total, qk_total, got_up, out = meet(vo_total, qk_total, got_up, out)
        state, gate_grad, down_grad, hidden_out, gain_rows = out
        got_vo, got_qk = net.send(to_leave(vo_total), col), net.send(to_leave(qk_total), col)

        def part_last():
            gains_grad = add_all(net, gain_rows, (lay.far, lay.col_axis))
            up_grad = jnp.concatenate(owned(total_up, got_up), 1)
            return lay.from_relative(grad_resid + scatter_end(state)), up_grad, gains_grad

        out = region(flag, part_last)
        got_vo, got_qk, (in_grad, up_grad, gains_grad) = meet(got_vo, got_qk, out)
        vo_pair = owned(vo_total, got_vo)
        qk_pair = owned(qk_total, got_qk)
        query_grad, key_grad, value_grad, out_grad_own = (
            jnp.concatenate([part[:, i * head_cols : (i + 1) * head_cols] for part in pair], 1)
            for pair in (qk_pair, vo_pair)
            for i in range(2)
        )
        return (
            hidden_out,
            in_grad,
            query_grad,
            key_grad,
            value_grad,
            out_grad_own,
            gate_grad,
            up_grad,
            down_grad,
            gains_grad,
        )

    return on_device


def solution(mesh):
    lay = Layout(mesh.shape["dp"], mesh.shape["tensor"])
    fine = Mesh(mesh.devices.reshape(lay.shape_of()), lay.dp_axes + lay.tensor_axes)
    tokens = P(lay.dp_axes + lay.tensor_axes, None)
    weights = P(lay.dp_axes, lay.tensor_axes)
    rows = P(lay.dp_axes)
    return jax.shard_map(
        block_program(lay),
        mesh=fine,
        in_specs=(tokens, tokens) + (weights,) * 7 + (P(), rows, rows),
        out_specs=(tokens, tokens) + (weights,) * 7 + (P(),),
        check_vma=False,
    )
```
